32 devices in a mesh: basis: 16 (over z, y, x), angle: 1, pol: 2 (over core).
Axes of the slice: x: 2, y: 2, z: 4, core: 2. Of those that a mesh axis runs over, the one named last changes fastest.
Arguments:
- adjoint: float32 [2, 16, 128, 2, 128], P('pol', 'angle', 'basis'), may hold values from -6 to 6
- currents: float32 [2, 16, 128, 2, 128], P('pol', 'angle', 'basis'), may hold values from -6 to 6
- radiation: float32 [2, 16, 128, 2, 128], P('pol', 'angle', 'basis'), may hold values from -6 to 6
- near_blocks: bfloat16 [128, 6, 2, 128, 128], P('basis'), may hold values from -0.15625 to 0.15625
- inverse_blocks: bfloat16 [128, 2, 128, 128], P('basis'), may hold values from -0.375 to 0.375
- col_device: int32 [128, 6], P('basis'), may hold values from 0 to 15, all different within a row; in each aligned block of 8 rows (0 to 7, 8 to 15, ...) at most 6 rows name the same one
- col_offset: int32 [128, 6], P('basis'), may hold values from 0 to 7
- box_of_block: int32 [128], P('basis'), may hold values from 0 to 63
- pair_rate: float32 [128, 6], P('basis'), may hold values from -4 to 4
Outputs:
- updated: float32 [2, 16, 128, 2, 128], P('pol', 'angle', 'basis')
- shape_grad: float32 [64], P('basis')
The draws below stay inside these ranges and needn't reach their ends.
Inputs may be any that keep to these rules, and one draw needn't show every extreme that they name: `col_device`: each row names 6 different devices; the rows of one basis device name any device at most 6 times, and in some devices' rows one device exactly 6 times.
All inputs are finite; a program needn't handle non-finite values.
Results may differ from the reference program's by a relative error of at most 0.0033.
Values sent between devices are 32-bit elements; how exact they have to be, the bound alone decides.
No kernel may reach another device: no remote copies, remote signals or barrier semaphores. Data moves between devices by JAX's collectives and lax.ppermute only.
A program may use at most 64 MiB of HBM per device.

```python
import math
import jax
import jax.numpy as jnp
import numpy as np
from jax import lax

B = 128
K = 6
NB_DEV = 8
CAP = 6
NBLK = 128
NBOX = 64
ANGLES = 16
N_BASIS = 16


def plant(drawn, own_key, least, high):
    longest = drawn.shape.index(max(drawn.shape))
    spots = []
    for shift in (0, 1):
        where = [jax.random.randint(jax.random.fold_in(own_key, axis), (), 0, length) for axis, length in enumerate(drawn.shape)]
        where[longest] = (where[longest] + shift) % drawn.shape[longest]
        spots.append(tuple(where))
    return drawn.at[spots[0]].set(least).at[spots[1]].set(high)


def levels(rng, shape, shards, least, top_value):
    level, own = 1.0, jax.random.fold_in(rng, 6)
    for axis_at, blocks in shards:
        draws = jnp.exp(jax.random.uniform(jax.random.fold_in(own, axis_at), (blocks,), jnp.float32, least / len(shards), top_value / len(shards)))
        level = level * jnp.repeat(draws, shape[axis_at] // blocks).reshape([-1 if axis == axis_at else 1 for axis in range(len(shape))])
    return level


def deal_out(own_key, own, number, rows, amount, top, limit, lean):
    order = jax.random.permutation(own_key, amount)
    heavy_load, common = load_shares(amount, rows * top, limit, lean, True), load_shares(amount, rows * top, limit, lean, False)
    places = jnp.arange(amount)

    def named(lengths, offset_by):
        used = int((lengths > 0).sum())
        fixed = max(1, used // 4)
        shifted = fixed + (places - fixed + offset_by * (used - fixed)) % max(1, amount - fixed)
        return jnp.zeros((amount,), jnp.int32).at[order[jnp.where(places < fixed, places, shifted)]].set(jnp.asarray(lengths, jnp.int32))

    lengths = jnp.where(number % 4 == 0, named(heavy_load, number // 4), named(common, number - number // 4 - 1))
    mixed = jax.random.permutation(jax.random.fold_in(own, 3), amount)
    donor, sink = mixed[0:amount // 2 * 2:2], mixed[1:amount // 2 * 2:2]
    margin = jnp.minimum(lengths[donor] - 1, limit - lengths[sink]) // 2
    margin = jnp.where((donor == order[0]) | (sink == order[0]) | (lengths[sink] == 0), 0, jnp.maximum(margin, 0))
    shifted = jax.random.randint(jax.random.fold_in(own, 4), (amount // 2,), 0, 1 << 20) % (margin + 1)
    lengths = lengths.at[donor].add(-shifted).at[sink].add(shifted)
    items = jnp.searchsorted(jnp.cumsum(lengths), jnp.arange(rows * top), side="right").astype(jnp.int32)
    grid = items.reshape(top, rows).T
    grid = grid[jax.random.permutation(jax.random.fold_in(own, 1), rows)]
    offset_by = jax.random.randint(jax.random.fold_in(own, 2), (rows, 1), 0, top)
    return jnp.take_along_axis(grid, (jnp.arange(top)[None, :] + offset_by) % top, axis=1)


def load_shares(amount, total, bound, slope, full):
    weights = [(1 << 20) // math.isqrt(grade ** slope) + 1 for grade in range(1, amount + 1)]
    largest = bound if full else min(bound, max(-(-total // amount), total * weights[0] // sum(weights)))
    least = 1 if total - largest >= amount - 1 else 0
    holding, rest = [largest] + [least] * (amount - 1), total - largest - least * (amount - 1)
    while rest > 0:
        movable = [i for i in range(1, amount) if holding[i] < largest] or [i for i in range(1, amount) if holding[i] < bound]
        whole, left = sum([weights[i] for i in movable]), rest
        for i in movable:
            more = min(bound - holding[i], max(1, left * weights[i] // whole), rest)
            holding[i] = holding[i] + more
            rest = rest - more
    return np.array(holding)


def noise(stream_key, dims, deviation, limit, shards=(), kind=jnp.bfloat16):
    values = jax.random.normal(stream_key, dims, jnp.float32) * deviation
    if len(shards) > 0:
        values = levels(stream_key, dims, shards, -0.22, 0.18) * values
    return jnp.clip(values, min=-limit, max=limit).astype(kind)


def setup_inputs(seed: int = 0) -> dict:
    key_of = jax.random.split(jax.random.key(seed), 10)
    adjoint = noise(key_of[0], (2, ANGLES, NBLK, 2, B), 1.0, 6.0, ((0, 2), (2, 16)), jnp.float32)
    currents = noise(key_of[1], (2, ANGLES, NBLK, 2, B), 1.0, 6.0, ((0, 2), (2, 16)), jnp.float32)
    radiation = noise(key_of[2], (2, ANGLES, NBLK, 2, B), 1.0, 6.0, ((0, 2), (2, 16)), jnp.float32)
    near_blocks = noise(key_of[3], (NBLK, K, 2, B, B), (2 * B * K) ** -0.5, 0.15625, ((0, 16),))
    inverse_blocks = noise(key_of[4], (NBLK, 2, B, B), (2 * B) ** -0.5, 0.375, ((0, 16),))
    col_device_keys = jax.random.split(jax.random.fold_in(key_of[5], 1), NBLK // NB_DEV)
    col_device_turns = jax.random.permutation(jax.random.fold_in(key_of[5], 3), NBLK // NB_DEV)
    col_device = jax.vmap(lambda own, number: deal_out(jax.random.fold_in(key_of[5], 2), own, number, NB_DEV, N_BASIS, K, CAP, 2))(col_device_keys, col_device_turns).reshape((NBLK, K))
    col_offset = plant(jax.random.randint(key_of[6], (NBLK, K), 0, NB_DEV), jax.random.fold_in(key_of[6], 1), 0, NB_DEV - 1).astype(jnp.int32)
    box_of_block = plant(jax.random.randint(key_of[7], (NBLK,), 0, NBOX), jax.random.fold_in(key_of[7], 1), 0, NBOX - 1).astype(jnp.int32)
    pair_rate = noise(key_of[8], (NBLK, K), 1.0, 4.0, ((0, 16),), jnp.float32)
    return {"adjoint": adjoint, "currents": currents, "radiation": radiation, "near_blocks": near_blocks, "inverse_blocks": inverse_blocks, "col_device": col_device, "col_offset": col_offset, "box_of_block": box_of_block, "pair_rate": pair_rate}


def conjugate_apply(matrices, vectors):
    highest = lax.Precision.HIGHEST
    real_part = jnp.einsum('nm,...n->...m', matrices[0], vectors[..., 0, :], precision=highest) + jnp.einsum('nm,...n->...m', matrices[1], vectors[..., 1, :], precision=highest)
    imag_part = jnp.einsum('nm,...n->...m', matrices[0], vectors[..., 1, :], precision=highest) - jnp.einsum('nm,...n->...m', matrices[1], vectors[..., 0, :], precision=highest)
    return jnp.stack([real_part, imag_part], axis=-2)

def reference(adjoint, currents, radiation, near_blocks, inverse_blocks, col_device, col_offset, box_of_block, pair_rate):
    highest = lax.Precision.HIGHEST
    norm_far = 1.0 / math.sqrt(NBLK * B)
    rad_real = radiation[:, :, :, 0, :]
    rad_imag = radiation[:, :, :, 1, :]
    cur_real = currents[:, :, :, 0, :]
    cur_imag = currents[:, :, :, 1, :]
    far_real = (lax.optimization_barrier(jnp.sum(rad_real * cur_real - rad_imag * cur_imag, axis=(2, 3))) * norm_far)[:, :, None, None]
    far_imag = (lax.optimization_barrier(jnp.sum(rad_real * cur_imag + rad_imag * cur_real, axis=(2, 3))) * norm_far)[:, :, None, None]
    source = jnp.stack([far_real * rad_real + far_imag * rad_imag, far_imag * rad_real - far_real * rad_imag], axis=3)
    rounded = lax.optimization_barrier(adjoint.astype(jnp.bfloat16)).astype(jnp.float32)
    columns = (col_device * NB_DEV + col_offset).astype(jnp.int32)

    def row_step(carry, row_index):
        totals, box_sums = carry
        matrices = near_blocks[row_index].astype(jnp.float32)
        vectors = lax.dynamic_index_in_dim(rounded, row_index, axis=2, keepdims=False)
        for slot_index in range(K):
            term = conjugate_apply(matrices[slot_index], vectors)
            column = columns[row_index, slot_index]
            totals = totals.at[:, :, column].add(term)
            beside = lax.dynamic_index_in_dim(currents, column, axis=2, keepdims=False)
            box_sums = box_sums.at[box_of_block[row_index]].add(pair_rate[row_index, slot_index] * jnp.sum(term * beside))
        return ((totals, box_sums), None)
    start = (jnp.zeros(source.shape, jnp.float32), jnp.zeros((NBOX,), jnp.float32))
    (totals, box_sums), _ = lax.scan(row_step, start, jnp.arange(NBLK, dtype=jnp.int32))
    residual = lax.optimization_barrier((source - totals).astype(jnp.bfloat16)).astype(jnp.float32)
    inverse = inverse_blocks.astype(jnp.float32)
    res_real = residual[:, :, :, 0, :]
    res_imag = residual[:, :, :, 1, :]
    upd_real = jnp.einsum('cnm,pacn->pacm', inverse[:, 0], res_real, precision=highest) + jnp.einsum('cnm,pacn->pacm', inverse[:, 1], res_imag, precision=highest)
    upd_imag = jnp.einsum('cnm,pacn->pacm', inverse[:, 0], res_imag, precision=highest) - jnp.einsum('cnm,pacn->pacm', inverse[:, 1], res_real, precision=highest)
    updated = adjoint + jnp.stack([upd_real, upd_imag], axis=3)
    shape_grad = box_sums * (-1.0 / math.sqrt(4 * B * ANGLES * K))
    return (updated, shape_grad)
```

```python
import functools
import math

import jax
import jax.numpy as jnp
from jax import lax
from jax.experimental import pallas as pl
from jax.experimental.pallas import tpu as pltpu
from jax.sharding import PartitionSpec as P

LOW = 4
LANES = 128
BOX_DEV = 4
VMEM_LIMIT = 48 * 1024 * 1024


def complex_rows(real, imag):
    return jnp.concatenate(
        [jnp.concatenate([real, imag], axis=1), jnp.concatenate([imag, -real], axis=1)], axis=0
    )


def fill_kernel(
    angles,
    slots,
    col_device_ref,
    col_offset_ref,
    box_ref,
    rate_ref,
    adjoint_ref,
    currents_ref,
    radiation_ref,
    near_ref,
    *out_refs,
):
    message_refs, current_rows_ref = out_refs[:LOW], out_refs[LOW]
    blocks, near_count = col_device_ref.shape
    stride = 2 * blocks
    me = lax.axis_index("basis")
    my_low = lax.rem(me, LOW)
    my_high = lax.div(me, LOW)
    for row in range(blocks):
        for part in range(2):
            current_rows_ref[row, pl.ds(part * angles, angles), :] = currents_ref[
                pl.ds(2 * row + part, angles, stride=stride), :
            ]
    count = angles * blocks
    rad_real = radiation_ref[pl.ds(0, count, stride=2), :]
    rad_imag = radiation_ref[pl.ds(1, count, stride=2), :]
    cur_real = currents_ref[pl.ds(0, count, stride=2), :]
    cur_imag = currents_ref[pl.ds(1, count, stride=2), :]
    far_real = jnp.sum((rad_real * cur_real - rad_imag * cur_imag).reshape(angles, blocks, LANES), axis=1)
    far_imag = jnp.sum((rad_real * cur_imag + rad_imag * cur_real).reshape(angles, blocks, LANES), axis=1)
    lane = lax.broadcasted_iota(jnp.int32, (angles, LANES), 1)
    far = jnp.where(lane == 0, jnp.sum(far_real, axis=1, keepdims=True), 0.0) + jnp.where(
        lane == 1, jnp.sum(far_imag, axis=1, keepdims=True), 0.0
    )
    spread = LANES // LOW
    lane8 = lax.broadcasted_iota(jnp.int32, (8, LANES), 1)
    sub8 = lax.broadcasted_iota(jnp.int32, (8, LANES), 0)
    table = jnp.zeros((8, LANES), jnp.float32)
    counts = [jnp.int32(0)] * LOW
    for row in range(blocks):
        real = adjoint_ref[pl.ds(2 * row, angles, stride=stride), :].astype(jnp.bfloat16)
        imag = adjoint_ref[pl.ds(2 * row + 1, angles, stride=stride), :].astype(jnp.bfloat16)
        left = complex_rows(real, imag)
        box = box_ref[row].astype(jnp.float32)
        for k in range(near_count):
            term = jnp.dot(left, near_ref[row * near_count + k], preferred_element_type=jnp.float32)
            device = col_device_ref[row, k]
            low = lax.bitwise_xor(lax.rem(device, LOW), my_low)
            high = lax.bitwise_xor(lax.div(device, LOW), my_high)
            place = high * blocks + col_offset_ref[row, k] + 1
            own_slot = jnp.int32(0)
            for e in range(LOW):
                here = low == e
                slot = jnp.where(here, jnp.minimum(counts[e], slots), slots)
                own_slot = jnp.where(here, counts[e], own_slot)
                counts[e] = counts[e] + here.astype(jnp.int32)
                message_refs[e][slot] = term
            entry = jnp.where(
                sub8 == 0, place.astype(jnp.float32), jnp.where(sub8 == 1, rate_ref[row, k], box)
            )
            table = jnp.where(lane8 == low * spread + own_slot, entry, table)
    for e in range(LOW):
        message_refs[e][slots, pl.ds(0, angles), :] = far
        message_refs[e][slots, pl.ds(angles, 8), :] = jnp.where(lane8 // spread == e, table, 0.0)


def sum_kernel(angles, slots, high_count, *refs):
    message_refs = refs[:LOW]
    current_refs = refs[LOW : LOW + high_count]
    out_refs = refs[LOW + high_count : LOW + 2 * high_count]
    grad_ref, acc_ref, cur_ref, prod_ref, table_ref, place_ref, sem = refs[LOW + 2 * high_count :]
    blocks = current_refs[0].shape[0]
    spread = LANES // LOW
    table = message_refs[0][slots, pl.ds(angles, 8), :]
    far = message_refs[0][slots, pl.ds(0, angles), :]
    for e in range(1, LOW):
        table = table + message_refs[e][slots, pl.ds(angles, 8), :]
        far = far + message_refs[e][slots, pl.ds(0, angles), :]
    table_ref[...] = table.astype(jnp.int32)
    copy = pltpu.make_async_copy(table_ref, place_ref, sem)
    copy.start()
    for d in range(high_count):
        cur_ref[pl.ds(d * blocks, blocks)] = current_refs[d][...]
    acc_ref[...] = jnp.zeros(acc_ref.shape, jnp.float32)
    prod_ref[...] = jnp.zeros(prod_ref.shape, jnp.float32)
    copy.wait()
    for e in range(LOW):
        for s in range(slots):
            place = place_ref[0, e * spread + s]
            used = place > 0
            at = jnp.maximum(place - 1, 0)
            term = jnp.where(used, message_refs[e][s], 0.0)
            acc_ref[at] = acc_ref[at] + term
            both = term * cur_ref[at]
            prod_ref[e * spread + s] = jnp.sum(both.reshape(2 * angles // 8, 8, LANES), axis=0)
    for d in range(high_count):
        for b in range(blocks):
            out_refs[d][pl.ds(b * 2 * angles, 2 * angles), :] = acc_ref[d * blocks + b]
        out_refs[d][pl.ds(blocks * 2 * angles, angles), :] = far
    highest = lax.Precision.HIGHEST
    contract_last = (((1,), (1,)), ((), ()))
    by_slot = jnp.sum(prod_ref[...], axis=1)
    values = lax.dot_general(
        jnp.ones((8, LANES), jnp.float32),
        by_slot,
        contract_last,
        precision=highest,
        preferred_element_type=jnp.float32,
    )
    boxes = grad_ref.shape[1]
    number = lax.broadcasted_iota(jnp.int32, (boxes, LANES), 0).astype(jnp.float32)
    rates = jnp.where(number == table[2:3, :], table[1:2, :], 0.0)
    grad_ref[...] = lax.dot_general(
        values, rates, contract_last, precision=highest, preferred_element_type=jnp.float32
    )


def update_kernel(angles, norm_far, high_count, *refs):
    sum_refs = refs[:high_count]
    adjoint_ref, radiation_ref, inverse_ref, out_ref = refs[high_count:]
    blocks = inverse_ref.shape[0]
    stride = 2 * blocks
    record = 2 * angles
    far = sum_refs[0][pl.ds(blocks * record, angles), :]
    for d in range(1, high_count):
        far = far + sum_refs[d][pl.ds(blocks * record, angles), :]
    far = far * norm_far
    far_real = jnp.broadcast_to(far[:, 0:1], (angles, LANES))
    far_imag = jnp.broadcast_to(far[:, 1:2], (angles, LANES))
    for block in range(blocks):
        rows_real = pl.ds(2 * block, angles, stride=stride)
        rows_imag = pl.ds(2 * block + 1, angles, stride=stride)
        total = sum_refs[0][pl.ds(block * record, record), :]
        for d in range(1, high_count):
            total = total + sum_refs[d][pl.ds(block * record, record), :]
        rad_real, rad_imag = radiation_ref[rows_real, :], radiation_ref[rows_imag, :]
        real = (far_real * rad_real + far_imag * rad_imag - total[:angles]).astype(jnp.bfloat16)
        imag = (far_imag * rad_real - far_real * rad_imag - total[angles:]).astype(jnp.bfloat16)
        step = jnp.dot(complex_rows(real, imag), inverse_ref[block], preferred_element_type=jnp.float32)
        out_ref[rows_real, :] = adjoint_ref[rows_real, :] + step[:angles]
        out_ref[rows_imag, :] = adjoint_ref[rows_imag, :] + step[angles:]


def on_device(
    adjoint,
    currents,
    radiation,
    near_blocks,
    inverse_blocks,
    col_device,
    col_offset,
    box_of_block,
    pair_rate,
):
    angles, blocks, unknowns = adjoint.shape[1], adjoint.shape[2], adjoint.shape[4]
    near_count = near_blocks.shape[1]
    pairs = blocks * near_count
    record = 2 * angles
    basis_count = lax.axis_size("basis")
    high_count = basis_count // LOW
    angles_all = angles * lax.axis_size("angle")
    boxes = BOX_DEV * basis_count
    slots = 2 * pairs // basis_count * high_count
    vmem = pl.BlockSpec(memory_space=pltpu.VMEM)
    smem = pl.BlockSpec(memory_space=pltpu.SMEM)
    params = pltpu.CompilerParams(vmem_limit_bytes=VMEM_LIMIT)

    def moved(value, bits):
        return lax.ppermute(value, "basis", [(i, i ^ bits) for i in range(basis_count)])

    flat = (angles * blocks * 2, unknowns)
    adjoint_rows = adjoint.reshape(flat)
    currents_rows = currents.reshape(flat)
    radiation_rows = radiation.reshape(flat)
    near = near_blocks.reshape(pairs, 2 * unknowns, unknowns)
    inverse = inverse_blocks.reshape(blocks, 2 * unknowns, unknowns)
    message = jax.ShapeDtypeStruct((slots + 1, record, unknowns), jnp.float32)
    current_shape = jax.ShapeDtypeStruct((blocks, record, unknowns), jnp.float32)
    *messages, own_currents = pl.pallas_call(
        functools.partial(fill_kernel, angles, slots),
        out_shape=[message] * LOW + [current_shape],
        in_specs=[smem] * 4 + [vmem] * 4,
        out_specs=[vmem] * (LOW + 1),
        compiler_params=params,
        name="fill",
    )(col_device, col_offset, box_of_block, pair_rate, adjoint_rows, currents_rows, radiation_rows, near)
    arrived = [messages[0]] + [moved(messages[e], e) for e in range(1, LOW)]
    beside = [own_currents] + [moved(own_currents, d * LOW) for d in range(1, high_count)]
    partial = jax.ShapeDtypeStruct((blocks * record + angles, unknowns), jnp.float32)
    box_lanes = -(-boxes // LANES) * LANES
    *sums, grad = pl.pallas_call(
        functools.partial(sum_kernel, angles, slots, high_count),
        out_shape=[partial] * high_count + [jax.ShapeDtypeStruct((8, box_lanes), jnp.float32)],
        in_specs=[vmem] * (LOW + high_count),
        out_specs=[vmem] * (high_count + 1),
        scratch_shapes=[
            pltpu.VMEM((high_count * blocks, record, unknowns), jnp.float32),
            pltpu.VMEM((high_count * blocks, record, unknowns), jnp.float32),
            pltpu.VMEM((LANES, 8, unknowns), jnp.float32),
            pltpu.VMEM((8, LANES), jnp.int32),
            pltpu.SMEM((8, LANES), jnp.int32),
            pltpu.SemaphoreType.DMA,
        ],
        compiler_params=params,
        name="sum",
    )(*arrived, *beside)
    totals = [sums[0]] + [moved(sums[d], d * LOW) for d in range(1, high_count)]
    updated = pl.pallas_call(
        functools.partial(update_kernel, angles, 1.0 / math.sqrt(blocks * basis_count * unknowns), high_count),
        out_shape=jax.ShapeDtypeStruct(flat, jnp.float32),
        in_specs=[vmem] * (high_count + 3),
        out_specs=vmem,
        compiler_params=params,
        name="update",
    )(*totals, adjoint_rows, radiation_rows, inverse)
    for bits in (range(1, LOW), range(LOW, basis_count, LOW)):
        grad = functools.reduce(jnp.add, [moved(grad, b) for b in bits], grad)
    for axis in ("angle", "pol"):
        size = lax.axis_size(axis)
        grad = functools.reduce(
            jnp.add,
            [lax.ppermute(grad, axis, [(i, i ^ b) for i in range(size)]) for b in range(1, size)],
            grad,
        )
    share = lax.dynamic_slice_in_dim(grad[0], lax.axis_index("basis") * BOX_DEV, BOX_DEV)
    shape_grad = share * (-1.0 / math.sqrt(4 * unknowns * angles_all * near_count))
    return (updated.reshape(adjoint.shape), shape_grad)


def solution(mesh):
    placed = (
        P("pol", "angle", "basis", None, None),
        P("pol", "angle", "basis", None, None),
        P("pol", "angle", "basis", None, None),
        P("basis", None, None, None, None),
        P("basis", None, None, None),
        P("basis", None),
        P("basis", None),
        P("basis"),
        P("basis", None),
    )
    return jax.shard_map(
        on_device,
        mesh=mesh,
        in_specs=placed,
        out_specs=(P("pol", "angle", "basis", None, None), P("basis")),
        check_vma=False,
    )
```

```python
import functools
import math

import jax
import jax.numpy as jnp
from jax import lax
from jax.experimental import pallas as pl
from jax.experimental.pallas import tpu as pltpu
from jax.sharding import PartitionSpec as P

LOW = 4
LANES = 128
BOX_DEV = 4
VMEM_LIMIT = 48 * 1024 * 1024


def cut(angles):
    sizes = [angles]
    return [(sum(sizes[:c]), size) for c, size in enumerate(sizes)]


def complex_rows(real, imag):
    return jnp.concatenate(
        [jnp.concatenate([real, imag], axis=1), jnp.concatenate([imag, -real], axis=1)], axis=0
    )


def fill_kernel(chunks, slots, *refs):
    whole_refs, refs = refs[:8], refs[8:]
    message_refs = [refs[c * LOW : (c + 1) * LOW] for c in range(len(chunks))]
    current_refs, refs = refs[len(chunks) * LOW : len(chunks) * (LOW + 1)], refs[len(chunks) * (LOW + 1) :]
    held_refs, (sems, near_sems) = refs[:8], refs[8:]
    (
        col_device_ref,
        col_offset_ref,
        box_ref,
        rate_ref,
        adjoint_ref,
        currents_ref,
        radiation_ref,
        near_ref,
    ) = held_refs
    blocks, near_count = col_device_ref.shape
    stride = 2 * blocks
    angles = adjoint_ref.shape[0] // stride
    copies = [
        pltpu.make_async_copy(whole_refs[i], held_refs[i], sems.at[i]) for i in (0, 1, 2, 3, 4, 5, 6)
    ]
    near_copies = [
        pltpu.make_async_copy(
            whole_refs[7].at[pl.ds(row * near_count, near_count)],
            near_ref.at[pl.ds(row * near_count, near_count)],
            near_sems.at[row],
        )
        for row in range(blocks)
    ]
    for copy in copies[:5] + near_copies[:2] + copies[5:] + near_copies[2:]:
        copy.start()
    me = lax.axis_index("basis")
    my_low = lax.rem(me, LOW)
    my_high = lax.div(me, LOW)
    spread = LANES // LOW
    lane8 = lax.broadcasted_iota(jnp.int32, (8, LANES), 1)
    sub8 = lax.broadcasted_iota(jnp.int32, (8, LANES), 0)
    table = jnp.zeros((8, LANES), jnp.float32)
    counts = [jnp.int32(0)] * LOW
    for copy in copies[:5]:
        copy.wait()
    for row in range(blocks):
        real = adjoint_ref[pl.ds(2 * row, angles, stride=stride), :].astype(jnp.bfloat16)
        imag = adjoint_ref[pl.ds(2 * row + 1, angles, stride=stride), :].astype(jnp.bfloat16)
        left = complex_rows(real, imag)
        box = box_ref[row].astype(jnp.float32)
        near_copies[row].wait()
        for k in range(near_count):
            term = jnp.dot(left, near_ref[row * near_count + k], preferred_element_type=jnp.float32)
            device = col_device_ref[row, k]
            low = lax.bitwise_xor(lax.rem(device, LOW), my_low)
            high = lax.bitwise_xor(lax.div(device, LOW), my_high)
            place = high * blocks + col_offset_ref[row, k] + 1
            own_slot = jnp.int32(0)
            for e in range(LOW):
                here = low == e
                slot = jnp.where(here, jnp.minimum(counts[e], slots), slots)
                own_slot = jnp.where(here, counts[e], own_slot)
                counts[e] = counts[e] + here.astype(jnp.int32)
                for c, (first, size) in enumerate(chunks):
                    message_refs[c][e][slot, pl.ds(0, size), :] = term[first : first + size]
                    message_refs[c][e][slot, pl.ds(size, size), :] = term[
                        angles + first : angles + first + size
                    ]
            entry = jnp.where(
                sub8 == 0, place.astype(jnp.float32), jnp.where(sub8 == 1, rate_ref[row, k], box)
            )
            table = jnp.where(lane8 == low * spread + own_slot, entry, table)
    for copy in copies[5:]:
        copy.wait()
    for row in range(blocks):
        for part in range(2):
            rows = currents_ref[pl.ds(2 * row + part, angles, stride=stride), :]
            for c, (first, size) in enumerate(chunks):
                current_refs[c][row, pl.ds(part * size, size), :] = rows[first : first + size]
    count = angles * blocks
    rad_real = radiation_ref[pl.ds(0, count, stride=2), :]
    rad_imag = radiation_ref[pl.ds(1, count, stride=2), :]
    cur_real = currents_ref[pl.ds(0, count, stride=2), :]
    cur_imag = currents_ref[pl.ds(1, count, stride=2), :]
    far_real = jnp.sum((rad_real * cur_real - rad_imag * cur_imag).reshape(angles, blocks, LANES), axis=1)
    far_imag = jnp.sum((rad_real * cur_imag + rad_imag * cur_real).reshape(angles, blocks, LANES), axis=1)
    lane = lax.broadcasted_iota(jnp.int32, (angles, LANES), 1)
    far = jnp.where(lane == 0, jnp.sum(far_real, axis=1, keepdims=True), 0.0) + jnp.where(
        lane == 1, jnp.sum(far_imag, axis=1, keepdims=True), 0.0
    )
    for e in range(LOW):
        mine = jnp.where(lane8 // spread == e, table, 0.0)
        extra = jnp.concatenate([far, mine], axis=0)
        size2 = 2 * chunks[0][1]
        for part in range(-(-extra.shape[0] // size2)):
            rows = extra[part * size2 : (part + 1) * size2]
            message_refs[0][e][slots + part, pl.ds(0, rows.shape[0]), :] = rows


def sum_kernel(angles, size, slots, high_count, first, last, *refs):
    message_refs, refs = refs[:LOW], refs[LOW:]
    current_refs, refs = refs[:high_count], refs[high_count:]
    if not first:
        (earlier_table_ref, earlier_ref), refs = refs[:2], refs[2:]
    out_refs, refs = refs[:high_count], refs[high_count:]
    if last:
        (grad_ref,), refs = refs[:1], refs[1:]
    else:
        (next_table_ref, next_ref), refs = refs[:2], refs[2:]
    acc_ref, cur_ref, prod_ref, table_ref, place_ref, sem = refs
    blocks = current_refs[0].shape[0]
    spread = LANES // LOW
    record = 2 * size
    if first:
        extra = None
        for e in range(LOW):
            parts = [message_refs[e][slots + part] for part in range(message_refs[e].shape[0] - slots)]
            own = jnp.concatenate(parts, axis=0) if len(parts) > 1 else parts[0]
            extra = own if extra is None else extra + own
        far, table = extra[:angles], extra[angles : angles + 8]
    else:
        table = earlier_table_ref[...]
    table_ref[...] = table.astype(jnp.int32)
    copy = pltpu.make_async_copy(table_ref, place_ref, sem)
    copy.start()
    for d in range(high_count):
        cur_ref[pl.ds(d * blocks, blocks)] = current_refs[d][...]
    acc_ref[...] = jnp.zeros(acc_ref.shape, jnp.float32)
    prod_ref[...] = jnp.zeros(prod_ref.shape, jnp.float32)
    copy.wait()
    for e in range(LOW):
        for s in range(slots):
            place = place_ref[0, e * spread + s]
            used = place > 0
            at = jnp.maximum(place - 1, 0)
            term = jnp.where(used, message_refs[e][s], 0.0)
            acc_ref[at] = acc_ref[at] + term
            both = term * cur_ref[at]
            prod_ref[e * spread + s] = jnp.sum(both.reshape(record // 8, 8, LANES), axis=0)
    for d in range(high_count):
        for b in range(blocks):
            out_refs[d][pl.ds(b * record, record), :] = acc_ref[d * blocks + b]
        if first:
            out_refs[d][pl.ds(blocks * record, angles), :] = far
    by_slot = jnp.sum(prod_ref[...], axis=1)
    if not first:
        by_slot = by_slot + earlier_ref[...]
    if not last:
        next_table_ref[...] = table
        next_ref[...] = by_slot
        return
    highest = lax.Precision.HIGHEST
    contract_last = (((1,), (1,)), ((), ()))
    values = lax.dot_general(
        jnp.ones((8, LANES), jnp.float32),
        by_slot,
        contract_last,
        precision=highest,
        preferred_element_type=jnp.float32,
    )
    boxes = grad_ref.shape[1]
    number = lax.broadcasted_iota(jnp.int32, (boxes, LANES), 0).astype(jnp.float32)
    rates = jnp.where(number == table[2:3, :], table[1:2, :], 0.0)
    grad_ref[...] = lax.dot_general(
        values, rates, contract_last, precision=highest, preferred_element_type=jnp.float32
    )


def update_kernel(chunks, angles, norm_far, high_count, *refs):
    sum_refs = [refs[c * high_count : (c + 1) * high_count] for c in range(len(chunks))]
    adjoint_ref, radiation_ref, inverse_ref, out_ref = refs[len(chunks) * high_count :]
    blocks = inverse_ref.shape[0]
    stride = 2 * blocks

    def total(c, start, rows):
        parts = [ref[pl.ds(start, rows), :] for ref in sum_refs[c]]
        return functools.reduce(jnp.add, parts)

    far = total(0, blocks * 2 * chunks[0][1], angles) * norm_far
    far_real = jnp.broadcast_to(far[:, 0:1], (angles, LANES))
    far_imag = jnp.broadcast_to(far[:, 1:2], (angles, LANES))
    for block in range(blocks):
        rows_real = pl.ds(2 * block, angles, stride=stride)
        rows_imag = pl.ds(2 * block + 1, angles, stride=stride)
        near_real = [total(c, block * 2 * size, size) for c, (_, size) in enumerate(chunks)]
        near_imag = [total(c, block * 2 * size + size, size) for c, (_, size) in enumerate(chunks)]
        near_real = jnp.concatenate(near_real, axis=0)
        near_imag = jnp.concatenate(near_imag, axis=0)
        rad_real, rad_imag = radiation_ref[rows_real, :], radiation_ref[rows_imag, :]
        real = (far_real * rad_real + far_imag * rad_imag - near_real).astype(jnp.bfloat16)
        imag = (far_imag * rad_real - far_real * rad_imag - near_imag).astype(jnp.bfloat16)
        step = jnp.dot(complex_rows(real, imag), inverse_ref[block], preferred_element_type=jnp.float32)
        out_ref[rows_real, :] = adjoint_ref[rows_real, :] + step[:angles]
        out_ref[rows_imag, :] = adjoint_ref[rows_imag, :] + step[angles:]


def on_device(
    adjoint,
    currents,
    radiation,
    near_blocks,
    inverse_blocks,
    col_device,
    col_offset,
    box_of_block,
    pair_rate,
):
    angles, blocks, unknowns = adjoint.shape[1], adjoint.shape[2], adjoint.shape[4]
    near_count = near_blocks.shape[1]
    pairs = blocks * near_count
    basis_count = lax.axis_size("basis")
    high_count = basis_count // LOW
    angles_all = angles * lax.axis_size("angle")
    boxes = BOX_DEV * basis_count
    slots = 2 * pairs // basis_count * high_count
    vmem = pl.BlockSpec(memory_space=pltpu.VMEM)
    smem = pl.BlockSpec(memory_space=pltpu.SMEM)
    params = pltpu.CompilerParams(vmem_limit_bytes=VMEM_LIMIT)

    def moved(value, bits):
        return lax.ppermute(value, "basis", [(i, i ^ bits) for i in range(basis_count)])

    flat = (angles * blocks * 2, unknowns)
    adjoint_rows = adjoint.reshape(flat)
    currents_rows = currents.reshape(flat)
    radiation_rows = radiation.reshape(flat)
    near = near_blocks.reshape(pairs, 2 * unknowns, unknowns)
    inverse = inverse_blocks.reshape(blocks, 2 * unknowns, unknowns)
    f32 = functools.partial(jax.ShapeDtypeStruct, dtype=jnp.float32)
    chunks = cut(angles)
    extra = [-(-(angles + 8) // (2 * chunks[0][1]))] + [1] * (len(chunks) - 1)
    filled = pl.pallas_call(
        functools.partial(fill_kernel, chunks, slots),
        out_shape=[f32((slots + more, 2 * size, unknowns)) for (_, size), more in zip(chunks, extra) for _ in range(LOW)]
        + [f32((blocks, 2 * size, unknowns)) for _, size in chunks],
        in_specs=[pl.BlockSpec(memory_space=pltpu.HBM)] * 8,
        out_specs=[vmem] * (len(chunks) * (LOW + 1)),
        scratch_shapes=[
            pltpu.SMEM(col_device.shape, jnp.int32),
            pltpu.SMEM(col_offset.shape, jnp.int32),
            pltpu.SMEM(box_of_block.shape, jnp.int32),
            pltpu.SMEM(pair_rate.shape, jnp.float32),
            pltpu.VMEM(flat, jnp.float32),
            pltpu.VMEM(flat, jnp.float32),
            pltpu.VMEM(flat, jnp.float32),
            pltpu.VMEM(near.shape, near.dtype),
            pltpu.SemaphoreType.DMA((7,)),
            pltpu.SemaphoreType.DMA((blocks,)),
        ],
        compiler_params=params,
        name="fill",
    )(
        *[
            pltpu.with_memory_space_constraint(whole, pltpu.HBM)
            for whole in (
                col_device,
                col_offset,
                box_of_block,
                pair_rate,
                adjoint_rows,
                currents_rows,
                radiation_rows,
                near,
            )
        ]
    )
    own_currents = filled[len(chunks) * LOW :]
    box_lanes = -(-boxes // LANES) * LANES
    totals, carried = [], []
    for c, (_, size) in enumerate(chunks):
        messages = filled[c * LOW : (c + 1) * LOW]
        arrived = [messages[0]] + [moved(messages[e], e) for e in range(1, LOW)]
        beside = [own_currents[c]] + [moved(own_currents[c], d * LOW) for d in range(1, high_count)]
        first, last = c == 0, c == len(chunks) - 1
        partial = f32((blocks * 2 * size + (angles if first else 0), unknowns))
        carry_shapes = [f32((8, box_lanes))] if last else [f32((8, LANES)), f32((LANES, unknowns))]
        sums_and_carry = pl.pallas_call(
            functools.partial(sum_kernel, angles, size, slots, high_count, first, last),
            out_shape=[partial] * high_count + carry_shapes,
            in_specs=[vmem] * (LOW + high_count + len(carried)),
            out_specs=[vmem] * (high_count + len(carry_shapes)),
            scratch_shapes=[
                pltpu.VMEM((high_count * blocks, 2 * size, unknowns), jnp.float32),
                pltpu.VMEM((high_count * blocks, 2 * size, unknowns), jnp.float32),
                pltpu.VMEM((LANES, 8, unknowns), jnp.float32),
                pltpu.VMEM((8, LANES), jnp.int32),
                pltpu.SMEM((8, LANES), jnp.int32),
                pltpu.SemaphoreType.DMA,
            ],
            compiler_params=params,
            name="sum",
        )(*arrived, *beside, *carried)
        sums, carried = sums_and_carry[:high_count], sums_and_carry[high_count:]
        totals += [sums[0]] + [moved(sums[d], d * LOW) for d in range(1, high_count)]
    (grad,) = carried
    norm_far = 1.0 / math.sqrt(blocks * basis_count * unknowns)
    updated = pl.pallas_call(
        functools.partial(update_kernel, chunks, angles, norm_far, high_count),
        out_shape=f32(flat),
        in_specs=[vmem] * (len(totals) + 3),
        out_specs=vmem,
        compiler_params=params,
        cost_estimate=pl.CostEstimate(flops=1 << 20, bytes_accessed=1 << 20, transcendentals=0),
        name="update",
    )(*totals, adjoint_rows, radiation_rows, inverse)
    everyone = ("basis", "pol")
    senders = basis_count * lax.axis_size("pol")
    gathered = lax.all_to_all(
        jnp.broadcast_to(grad[:1], (senders, 1, box_lanes)), everyone, split_axis=0, concat_axis=0
    )
    total_grad = jnp.sum(gathered[:, 0], axis=0)
    if lax.axis_size("angle") > 1:
        total_grad = lax.psum(total_grad, "angle")
    share = lax.dynamic_slice_in_dim(total_grad, lax.axis_index("basis") * BOX_DEV, BOX_DEV)
    shape_grad = share * (-1.0 / math.sqrt(4 * unknowns * angles_all * near_count))
    return (updated.reshape(adjoint.shape), shape_grad)


def solution(mesh):
    placed = (
        P("pol", "angle", "basis", None, None),
        P("pol", "angle", "basis", None, None),
        P("pol", "angle", "basis", None, None),
        P("basis", None, None, None, None),
        P("basis", None, None, None),
        P("basis", None),
        P("basis", None),
        P("basis"),
        P("basis", None),
    )
    return jax.shard_map(
        on_device,
        mesh=mesh,
        in_specs=placed,
        out_specs=(P("pol", "angle", "basis", None, None), P("basis")),
        check_vma=False,
    )
```

```python
import functools
import math

import jax
import jax.numpy as jnp
from jax import lax
from jax.experimental import pallas as pl
from jax.experimental.pallas import tpu as pltpu
from jax.sharding import PartitionSpec as P

LOW = 4
LANES = 128
BOX_DEV = 4
VMEM_LIMIT = 48 * 1024 * 1024


def complex_rows(real, imag):
    return jnp.concatenate(
        [jnp.concatenate([real, imag], axis=1), jnp.concatenate([imag, -real], axis=1)], axis=0
    )


def fill_kernel(slots, *refs):
    whole_refs, message_refs, current_rows_ref = refs[:8], refs[8 : 8 + LOW], refs[8 + LOW]
    *held_refs, sems, near_sems = refs[9 + LOW :]
    (
        col_device_ref,
        col_offset_ref,
        box_ref,
        rate_ref,
        adjoint_ref,
        currents_ref,
        radiation_ref,
        near_ref,
    ) = held_refs
    blocks, near_count = col_device_ref.shape
    stride = 2 * blocks
    angles = adjoint_ref.shape[0] // stride
    copies = [pltpu.make_async_copy(whole_refs[i], held_refs[i], sems.at[i]) for i in range(7)]
    near_copies = [
        pltpu.make_async_copy(
            whole_refs[7].at[pl.ds(row * near_count, near_count)],
            near_ref.at[pl.ds(row * near_count, near_count)],
            near_sems.at[row],
        )
        for row in range(blocks)
    ]
    for copy in copies[4:5] + near_copies[:1] + copies[:4] + near_copies[1:] + copies[5:]:
        copy.start()
    me = lax.axis_index("basis")
    my_low = lax.rem(me, LOW)
    my_high = lax.div(me, LOW)
    spread = LANES // LOW
    lane8 = lax.broadcasted_iota(jnp.int32, (8, LANES), 1)
    sub8 = lax.broadcasted_iota(jnp.int32, (8, LANES), 0)
    table = jnp.zeros((8, LANES), jnp.float32)
    counts = [jnp.int32(0)] * LOW
    for copy in copies[:5]:
        copy.wait()
    for row in range(blocks):
        real = adjoint_ref[pl.ds(2 * row, angles, stride=stride), :].astype(jnp.bfloat16)
        imag = adjoint_ref[pl.ds(2 * row + 1, angles, stride=stride), :].astype(jnp.bfloat16)
        left = complex_rows(real, imag)
        box = box_ref[row].astype(jnp.float32)
        near_copies[row].wait()
        for k in range(near_count):
            term = jnp.dot(left, near_ref[row * near_count + k], preferred_element_type=jnp.float32)
            device = col_device_ref[row, k]
            low = lax.bitwise_xor(lax.rem(device, LOW), my_low)
            high = lax.bitwise_xor(lax.div(device, LOW), my_high)
            place = high * blocks + col_offset_ref[row, k] + 1
            own_slot = jnp.int32(0)
            for e in range(LOW):
                here = low == e
                slot = jnp.where(here, jnp.minimum(counts[e], slots), slots)
                own_slot = jnp.where(here, counts[e], own_slot)
                counts[e] = counts[e] + here.astype(jnp.int32)
                message_refs[e][slot] = term
            entry = jnp.where(
                sub8 == 0, place.astype(jnp.float32), jnp.where(sub8 == 1, rate_ref[row, k], box)
            )
            table = jnp.where(lane8 == low * spread + own_slot, entry, table)
    for copy in copies[5:]:
        copy.wait()
    for row in range(blocks):
        for part in range(2):
            current_rows_ref[row, pl.ds(part * angles, angles), :] = currents_ref[
                pl.ds(2 * row + part, angles, stride=stride), :
            ]
    count = angles * blocks
    rad_real = radiation_ref[pl.ds(0, count, stride=2), :]
    rad_imag = radiation_ref[pl.ds(1, count, stride=2), :]
    cur_real = currents_ref[pl.ds(0, count, stride=2), :]
    cur_imag = currents_ref[pl.ds(1, count, stride=2), :]
    far_real = jnp.sum((rad_real * cur_real - rad_imag * cur_imag).reshape(angles, blocks, LANES), axis=1)
    far_imag = jnp.sum((rad_real * cur_imag + rad_imag * cur_real).reshape(angles, blocks, LANES), axis=1)
    lane = lax.broadcasted_iota(jnp.int32, (angles, LANES), 1)
    far = jnp.where(lane == 0, jnp.sum(far_real, axis=1, keepdims=True), 0.0) + jnp.where(
        lane == 1, jnp.sum(far_imag, axis=1, keepdims=True), 0.0
    )
    for e in range(LOW):
        message_refs[e][slots, pl.ds(0, angles), :] = far
        message_refs[e][slots, pl.ds(angles, 8), :] = jnp.where(lane8 // spread == e, table, 0.0)


def add_slots(message_refs, first, slots, tables, acc_ref, cur_ref, prod_ref, table_ref, place_ref, sem):
    spread = LANES // LOW
    table_ref[...] = tables.astype(jnp.int32)
    copy = pltpu.make_async_copy(table_ref, place_ref, sem)
    copy.start()
    prod_ref[...] = jnp.zeros(prod_ref.shape, jnp.float32)
    copy.wait()
    for i, message_ref in enumerate(message_refs):
        for s in range(slots):
            place = place_ref[0, (first + i) * spread + s]
            at = jnp.maximum(place - 1, 0)
            term = jnp.where(place > 0, message_ref[s], 0.0)
            acc_ref[at] = acc_ref[at] + term
            both = term * cur_ref[at]
            prod_ref[i * spread + s] = jnp.sum(both.reshape(-1, 8, LANES), axis=0)


def sum_first_kernel(slots, high_count, *refs):
    message_refs, current_refs = refs[: LOW // 2], refs[LOW // 2 : LOW // 2 + high_count]
    acc_ref, cur_ref, extra_ref, by_slot_ref, prod_ref, *tables = refs[LOW // 2 + high_count :]
    blocks, record = current_refs[0].shape[:2]
    extra = message_refs[0][slots]
    for message_ref in message_refs[1:]:
        extra = extra + message_ref[slots]
    for d in range(high_count):
        cur_ref[pl.ds(d * blocks, blocks)] = current_refs[d][...]
    acc_ref[...] = jnp.zeros(acc_ref.shape, jnp.float32)
    own = extra[record // 2 : record // 2 + 8]
    add_slots(message_refs, 0, slots, own, acc_ref, cur_ref, prod_ref, *tables)
    extra_ref[...] = extra
    by_slot_ref[...] = jnp.sum(prod_ref[...], axis=1)


def sum_last_kernel(slots, high_count, blocks, *refs):
    message_refs, refs = refs[: LOW // 2], refs[LOW // 2 :]
    (first_ref, cur_ref, first_extra_ref, first_by_slot_ref), refs = refs[:4], refs[4:]
    out_refs, (grad_ref, acc_ref, prod_ref, *tables) = refs[:high_count], refs[high_count:]
    record = cur_ref.shape[1]
    angles = record // 2
    extra = message_refs[0][slots]
    for message_ref in message_refs[1:]:
        extra = extra + message_ref[slots]
    own = extra[angles : angles + 8]
    extra = extra + first_extra_ref[...]
    acc_ref[...] = first_ref[...]
    add_slots(message_refs, LOW // 2, slots, own, acc_ref, cur_ref, prod_ref, *tables)
    for d in range(high_count):
        for b in range(blocks):
            out_refs[d][pl.ds(b * record, record), :] = acc_ref[d * blocks + b]
        out_refs[d][pl.ds(blocks * record, angles), :] = extra[:angles]
    table = extra[angles : angles + 8]
    by_slot = jnp.concatenate([first_by_slot_ref[...], jnp.sum(prod_ref[...], axis=1)], axis=0)
    by_pair = jnp.transpose(table)
    shares = by_pair[:, 1:2] * jnp.sum(by_slot, axis=1, keepdims=True)
    senders, boxes = grad_ref.shape
    number = lax.broadcasted_iota(jnp.int32, (LANES, boxes), 1).astype(jnp.float32)
    box_sums = jnp.sum(jnp.where(by_pair[:, 2:3] == number, shares, 0.0), axis=0, keepdims=True)
    grad_ref[...] = jnp.broadcast_to(box_sums, (senders, boxes))


def update_kernel(angles, norm_far, high_count, *refs):
    sum_refs = refs[:high_count]
    adjoint_ref, radiation_ref, inverse_ref, out_ref = refs[high_count:]
    blocks = inverse_ref.shape[0]
    stride = 2 * blocks
    record = 2 * angles

    def total(start, rows):
        return functools.reduce(jnp.add, [ref[pl.ds(start, rows), :] for ref in sum_refs])

    far = total(blocks * record, angles) * norm_far
    far_real = jnp.broadcast_to(far[:, 0:1], (angles, LANES))
    far_imag = jnp.broadcast_to(far[:, 1:2], (angles, LANES))
    for block in range(blocks):
        rows_real = pl.ds(2 * block, angles, stride=stride)
        rows_imag = pl.ds(2 * block + 1, angles, stride=stride)
        near = total(block * record, record)
        rad_real, rad_imag = radiation_ref[rows_real, :], radiation_ref[rows_imag, :]
        real = (far_real * rad_real + far_imag * rad_imag - near[:angles]).astype(jnp.bfloat16)
        imag = (far_imag * rad_real - far_real * rad_imag - near[angles:]).astype(jnp.bfloat16)
        step = jnp.dot(complex_rows(real, imag), inverse_ref[block], preferred_element_type=jnp.float32)
        out_ref[rows_real, :] = adjoint_ref[rows_real, :] + step[:angles]
        out_ref[rows_imag, :] = adjoint_ref[rows_imag, :] + step[angles:]


def on_device(
    adjoint,
    currents,
    radiation,
    near_blocks,
    inverse_blocks,
    col_device,
    col_offset,
    box_of_block,
    pair_rate,
):
    angles, blocks, unknowns = adjoint.shape[1], adjoint.shape[2], adjoint.shape[4]
    near_count = near_blocks.shape[1]
    pairs = blocks * near_count
    record = 2 * angles
    basis_count = lax.axis_size("basis")
    high_count = basis_count // LOW
    angles_all = angles * lax.axis_size("angle")
    boxes = BOX_DEV * basis_count
    slots = 2 * pairs // basis_count * high_count
    vmem = pl.BlockSpec(memory_space=pltpu.VMEM)
    params = pltpu.CompilerParams(vmem_limit_bytes=VMEM_LIMIT)

    def moved(value, bits):
        return lax.ppermute(value, "basis", [(i, i ^ bits) for i in range(basis_count)])

    flat = (angles * blocks * 2, unknowns)
    adjoint_rows = adjoint.reshape(flat)
    currents_rows = currents.reshape(flat)
    radiation_rows = radiation.reshape(flat)
    near = near_blocks.reshape(pairs, 2 * unknowns, unknowns)
    inverse = inverse_blocks.reshape(blocks, 2 * unknowns, unknowns)
    f32 = functools.partial(jax.ShapeDtypeStruct, dtype=jnp.float32)
    message = f32((slots + 1, record, unknowns))
    inputs = (
        col_device,
        col_offset,
        box_of_block,
        pair_rate,
        adjoint_rows,
        currents_rows,
        radiation_rows,
        near,
    )
    *messages, own_currents = pl.pallas_call(
        functools.partial(fill_kernel, slots),
        out_shape=[message] * LOW + [f32((blocks, record, unknowns))],
        in_specs=[pl.BlockSpec(memory_space=pltpu.HBM)] * len(inputs),
        out_specs=[vmem] * (LOW + 1),
        scratch_shapes=[pltpu.SMEM(whole.shape, whole.dtype) for whole in inputs[:4]]
        + [pltpu.VMEM(whole.shape, whole.dtype) for whole in inputs[4:]]
        + [pltpu.SemaphoreType.DMA((7,)), pltpu.SemaphoreType.DMA((blocks,))],
        compiler_params=params,
        name="fill",
    )(*[pltpu.with_memory_space_constraint(whole, pltpu.HBM) for whole in inputs])
    arrived = [messages[0]] + [moved(messages[e], e) for e in range(1, LOW)]
    beside = [own_currents] + [moved(own_currents, d * LOW) for d in range(1, high_count)]
    columns = f32((high_count * blocks, record, unknowns))
    half = LANES // 2
    tables = [
        pltpu.VMEM((half, 8, unknowns), jnp.float32),
        pltpu.VMEM((8, LANES), jnp.int32),
        pltpu.SMEM((8, LANES), jnp.int32),
        pltpu.SemaphoreType.DMA,
    ]
    first_sums = pl.pallas_call(
        functools.partial(sum_first_kernel, slots, high_count),
        out_shape=[columns, columns, f32((record, unknowns)), f32((half, unknowns))],
        in_specs=[vmem] * (LOW // 2 + high_count),
        out_specs=[vmem] * 4,
        scratch_shapes=tables,
        compiler_params=params,
        name="sum_first",
    )(*arrived[: LOW // 2], *beside)
    partial = f32((blocks * record + angles, unknowns))
    box_lanes = -(-boxes // LANES) * LANES
    everyone = ("basis", "pol")
    senders = basis_count * lax.axis_size("pol")
    *sums, grad = pl.pallas_call(
        functools.partial(sum_last_kernel, slots, high_count, blocks),
        out_shape=[partial] * high_count + [f32((senders, box_lanes))],
        in_specs=[vmem] * (LOW // 2 + 4),
        out_specs=[vmem] * (high_count + 1),
        scratch_shapes=[pltpu.VMEM(columns.shape, jnp.float32)] + tables,
        compiler_params=params,
        name="sum_last",
    )(*arrived[LOW // 2 :], *first_sums)
    totals = [sums[0]] + [moved(sums[d], d * LOW) for d in range(1, high_count)]
    norm_far = 1.0 / math.sqrt(blocks * basis_count * unknowns)
    updated = pl.pallas_call(
        functools.partial(update_kernel, angles, norm_far, high_count),
        out_shape=f32(flat),
        in_specs=[vmem] * (high_count + 3),
        out_specs=vmem,
        compiler_params=params,
        name="update",
    )(*totals, adjoint_rows, radiation_rows, inverse)
    grad = grad.reshape(senders, 1, box_lanes)
    gathered = lax.all_to_all(grad, everyone, split_axis=0, concat_axis=0)
    gathered, updated = lax.optimization_barrier((gathered, updated))
    total_grad = jnp.sum(gathered[:, 0], axis=0)
    if lax.axis_size("angle") > 1:
        total_grad = lax.psum(total_grad, "angle")
    share = lax.dynamic_slice_in_dim(total_grad, lax.axis_index("basis") * BOX_DEV, BOX_DEV)
    shape_grad = share * (-1.0 / math.sqrt(4 * unknowns * angles_all * near_count))
    return (updated.reshape(adjoint.shape), shape_grad)


def solution(mesh):
    placed = (
        P("pol", "angle", "basis", None, None),
        P("pol", "angle", "basis", None, None),
        P("pol", "angle", "basis", None, None),
        P("basis", None, None, None, None),
        P("basis", None, None, None),
        P("basis", None),
        P("basis", None),
        P("basis"),
        P("basis", None),
    )
    return jax.shard_map(
        on_device,
        mesh=mesh,
        in_specs=placed,
        out_specs=(P("pol", "angle", "basis", None, None), P("basis")),
        check_vma=False,
    )
```

```python
import functools
import math

import jax
import jax.numpy as jnp
from jax import lax
from jax.experimental import pallas as pl
from jax.experimental.pallas import tpu as pltpu
from jax.sharding import PartitionSpec as P

LOW = 4
LANES = 128
BOX_DEV = 4
FAR_ROW = 3
VMEM_LIMIT = 48 * 1024 * 1024


def complex_rows(real, imag):
    return jnp.concatenate(
        [jnp.concatenate([real, imag], axis=1), jnp.concatenate([imag, -real], axis=1)], axis=0
    )


def fill_kernel(slots, *refs):
    whole_refs, message_refs, current_rows_ref = refs[:8], refs[8 : 8 + LOW], refs[8 + LOW]
    *held_refs, buffer_ref, sems, near_sems = refs[9 + LOW :]
    (
        col_device_ref,
        col_offset_ref,
        box_ref,
        rate_ref,
        adjoint_ref,
        currents_ref,
        radiation_ref,
        near_ref,
    ) = held_refs
    blocks, near_count = col_device_ref.shape
    stride = 2 * blocks
    angles = adjoint_ref.shape[0] // stride
    record = 2 * angles
    copies = [pltpu.make_async_copy(whole_refs[i], held_refs[i], sems.at[i]) for i in range(7)]
    near_copies = [
        pltpu.make_async_copy(
            whole_refs[7].at[pl.ds(row * near_count, near_count)],
            near_ref.at[pl.ds(row * near_count, near_count)],
            near_sems.at[row],
        )
        for row in range(blocks)
    ]
    for copy in copies[4:5] + near_copies[:1] + copies[:4] + near_copies[1:] + copies[5:]:
        copy.start()
    me = lax.axis_index("basis")
    my_low = lax.rem(me, LOW)
    my_high = lax.div(me, LOW)
    spread = LANES // LOW
    lane8 = lax.broadcasted_iota(jnp.int32, (8, LANES), 1)
    sub8 = lax.broadcasted_iota(jnp.int32, (8, LANES), 0)
    table = jnp.zeros((8, LANES), jnp.float32)
    counts = [jnp.int32(0)] * LOW
    for copy in copies[:5]:
        copy.wait()
    for row in range(blocks):
        real = adjoint_ref[pl.ds(2 * row, angles, stride=stride), :].astype(jnp.bfloat16)
        imag = adjoint_ref[pl.ds(2 * row + 1, angles, stride=stride), :].astype(jnp.bfloat16)
        left = complex_rows(real, imag)
        box = box_ref[row].astype(jnp.float32)
        near_copies[row].wait()
        for first in range(0, near_count, 1):
            some = range(first, min(first + 1, near_count))
            right = jnp.concatenate([near_ref[row * near_count + k] for k in some], axis=1)
            terms = jnp.dot(left, right, preferred_element_type=jnp.float32)
            for k in some:
                device = col_device_ref[row, k]
                low = lax.bitwise_xor(lax.rem(device, LOW), my_low)
                high = lax.bitwise_xor(lax.div(device, LOW), my_high)
                place = high * blocks + col_offset_ref[row, k] + 1
                slot = jnp.int32(0)
                for e in range(LOW):
                    here = low == e
                    slot = jnp.where(here, counts[e], slot)
                    counts[e] = counts[e] + here.astype(jnp.int32)
                slot = jnp.minimum(slot, slots - 1)
                buffer_ref[low * slots + slot] = terms[:, (k - first) * LANES : (k - first + 1) * LANES]
                entry = jnp.where(
                    sub8 == 0, place.astype(jnp.float32), jnp.where(sub8 == 1, rate_ref[row, k], box)
                )
                table = jnp.where(lane8 == low * spread + slot, entry, table)
    for copy in copies[5:]:
        copy.wait()
    for row in range(blocks):
        for part in range(2):
            current_rows_ref[row, pl.ds(part * angles, angles), :] = currents_ref[
                pl.ds(2 * row + part, angles, stride=stride), :
            ]
    count = angles * blocks
    rad_real = radiation_ref[pl.ds(0, count, stride=2), :]
    rad_imag = radiation_ref[pl.ds(1, count, stride=2), :]
    cur_real = currents_ref[pl.ds(0, count, stride=2), :]
    cur_imag = currents_ref[pl.ds(1, count, stride=2), :]
    far_real = jnp.sum((rad_real * cur_real - rad_imag * cur_imag).reshape(angles, blocks, LANES), axis=1)
    far_imag = jnp.sum((rad_real * cur_imag + rad_imag * cur_real).reshape(angles, blocks, LANES), axis=1)
    lane = lax.broadcasted_iota(jnp.int32, (angles, LANES), 1)
    angle = lax.broadcasted_iota(jnp.int32, (angles, LANES), 0)
    far = jnp.where(lane == angle, jnp.sum(far_real, axis=1, keepdims=True), 0.0) + jnp.where(
        lane == angle + angles, jnp.sum(far_imag, axis=1, keepdims=True), 0.0
    )
    far = jnp.broadcast_to(jnp.sum(far, axis=0, keepdims=True), (8, LANES))
    for e in range(LOW):
        for s in range(slots):
            message_refs[e][pl.ds(s * record, record), :] = buffer_ref[e * slots + s]
        mine = jnp.where(lane8 // spread == e, table, 0.0)
        message_refs[e][pl.ds(slots * record, 8), :] = jnp.where(sub8 == FAR_ROW, far, mine)


def add_slots(message_refs, first, slots, boxes, table, scratch_refs):
    acc_ref, cur_ref, prod_ref, table_ref, place_ref, sem = scratch_refs
    spread = LANES // LOW
    record = cur_ref.shape[1]
    table_ref[...] = table.astype(jnp.int32)
    copy = pltpu.make_async_copy(table_ref, place_ref, sem)
    copy.start()
    prod_ref[...] = jnp.zeros(prod_ref.shape, jnp.float32)
    count = len(message_refs) * spread
    by_pair = jnp.transpose(table)[first * spread : first * spread + count]
    number = lax.broadcasted_iota(jnp.int32, (count, boxes), 1).astype(jnp.float32)
    rates = jnp.where(by_pair[:, 2:3] == number, by_pair[:, 1:2], 0.0)
    copy.wait()
    for i, message_ref in enumerate(message_refs):
        for s in range(slots):
            place = place_ref[0, (first + i) * spread + s]
            at = jnp.maximum(place - 1, 0)
            term = jnp.where(place > 0, message_ref[pl.ds(s * record, record), :], 0.0)
            acc_ref[at] = acc_ref[at] + term
            both = term * cur_ref[at]
            prod_ref[i * spread + s] = jnp.sum(both.reshape(-1, 8, LANES), axis=0)
    by_slot = jnp.sum(jnp.sum(prod_ref[...], axis=1), axis=1, keepdims=True)
    return jnp.sum((rates * by_slot).reshape(count // 8, 8, boxes), axis=0)


def sum_first_kernel(slots, high_count, *refs):
    message_refs, current_refs = refs[: LOW // 2], refs[LOW // 2 : LOW // 2 + high_count]
    acc_ref, cur_ref, extra_ref, share_ref, *scratch_refs = refs[LOW // 2 + high_count :]
    blocks, record = current_refs[0].shape[:2]
    extra = functools.reduce(jnp.add, [ref[pl.ds(slots * record, 8), :] for ref in message_refs])
    for d in range(high_count):
        cur_ref[pl.ds(d * blocks, blocks)] = current_refs[d][...]
    acc_ref[...] = jnp.zeros(acc_ref.shape, jnp.float32)
    share_ref[...] = add_slots(message_refs, 0, slots, share_ref.shape[1], extra, (acc_ref, cur_ref, *scratch_refs))
    extra_ref[...] = extra


def sum_last_kernel(slots, high_count, blocks, *refs):
    message_refs, refs = refs[: LOW // 2], refs[LOW // 2 :]
    (first_ref, cur_ref, first_extra_ref, first_share_ref), refs = refs[:4], refs[4:]
    out_refs, (grad_ref, acc_ref, *scratch_refs) = refs[:high_count], refs[high_count:]
    record = cur_ref.shape[1]
    extra = functools.reduce(jnp.add, [ref[pl.ds(slots * record, 8), :] for ref in message_refs])
    acc_ref[...] = first_ref[...]
    share = add_slots(message_refs, LOW // 2, slots, grad_ref.shape[2], extra, (acc_ref, cur_ref, *scratch_refs))
    box_sums = jnp.sum(share + first_share_ref[...], axis=0, keepdims=True)
    grad_ref[...] = jnp.broadcast_to(box_sums[None], grad_ref.shape)
    extra = extra + first_extra_ref[...]
    for d in range(high_count):
        for b in range(blocks):
            out_refs[d][pl.ds(b * record, record), :] = acc_ref[d * blocks + b]
        for row in range(blocks * record, out_refs[d].shape[0], 8):
            out_refs[d][pl.ds(row, 8), :] = extra


def update_kernel(angles, norm_far, high_count, *refs):
    sum_refs = refs[:high_count]
    adjoint_ref, radiation_ref, inverse_ref, out_ref = refs[high_count:]
    blocks = inverse_ref.shape[0]
    stride = 2 * blocks
    record = 2 * angles

    def total(start, rows):
        return functools.reduce(jnp.add, [ref[pl.ds(start, rows), :] for ref in sum_refs])

    far = total(blocks * record, 8)[FAR_ROW : FAR_ROW + 1] * norm_far
    lane = lax.broadcasted_iota(jnp.int32, (angles, LANES), 1)
    angle = lax.broadcasted_iota(jnp.int32, (angles, LANES), 0)
    far_real = jnp.sum(jnp.where(lane == angle, far, 0.0), axis=1, keepdims=True)
    far_imag = jnp.sum(jnp.where(lane == angle + angles, far, 0.0), axis=1, keepdims=True)
    far_real = jnp.broadcast_to(far_real, (angles, LANES))
    far_imag = jnp.broadcast_to(far_imag, (angles, LANES))
    for block in range(blocks):
        rows_real = pl.ds(2 * block, angles, stride=stride)
        rows_imag = pl.ds(2 * block + 1, angles, stride=stride)
        near = total(block * record, record)
        rad_real, rad_imag = radiation_ref[rows_real, :], radiation_ref[rows_imag, :]
        real = (far_real * rad_real + far_imag * rad_imag - near[:angles]).astype(jnp.bfloat16)
        imag = (far_imag * rad_real - far_real * rad_imag - near[angles:]).astype(jnp.bfloat16)
        step = jnp.dot(complex_rows(real, imag), inverse_ref[block], preferred_element_type=jnp.float32)
        out_ref[rows_real, :] = adjoint_ref[rows_real, :] + step[:angles]
        out_ref[rows_imag, :] = adjoint_ref[rows_imag, :] + step[angles:]


def on_device(
    adjoint,
    currents,
    radiation,
    near_blocks,
    inverse_blocks,
    col_device,
    col_offset,
    box_of_block,
    pair_rate,
):
    angles, blocks, unknowns = adjoint.shape[1], adjoint.shape[2], adjoint.shape[4]
    near_count = near_blocks.shape[1]
    pairs = blocks * near_count
    record = 2 * angles
    basis_count = lax.axis_size("basis")
    high_count = basis_count // LOW
    angles_all = angles * lax.axis_size("angle")
    boxes = BOX_DEV * basis_count
    slots = 2 * pairs // basis_count * high_count
    vmem = pl.BlockSpec(memory_space=pltpu.VMEM)
    params = pltpu.CompilerParams(vmem_limit_bytes=VMEM_LIMIT)

    def moved(value, bits):
        return lax.ppermute(value, "basis", [(i, i ^ bits) for i in range(basis_count)])

    flat = (angles * blocks * 2, unknowns)
    adjoint_rows = adjoint.reshape(flat)
    currents_rows = currents.reshape(flat)
    radiation_rows = radiation.reshape(flat)
    near = near_blocks.reshape(pairs, 2 * unknowns, unknowns)
    inverse = inverse_blocks.reshape(blocks, 2 * unknowns, unknowns)
    f32 = functools.partial(jax.ShapeDtypeStruct, dtype=jnp.float32)
    message = f32((slots * record + 8, unknowns))
    inputs = (
        col_device,
        col_offset,
        box_of_block,
        pair_rate,
        adjoint_rows,
        currents_rows,
        radiation_rows,
        near,
    )
    *messages, own_currents = pl.pallas_call(
        functools.partial(fill_kernel, slots),
        out_shape=[message] * LOW + [f32((blocks, record, unknowns))],
        in_specs=[pl.BlockSpec(memory_space=pltpu.HBM)] * len(inputs),
        out_specs=[vmem] * (LOW + 1),
        scratch_shapes=[pltpu.SMEM(whole.shape, whole.dtype) for whole in inputs[:4]]
        + [pltpu.VMEM(whole.shape, whole.dtype) for whole in inputs[4:]]
        + [pltpu.VMEM((LOW * slots, record, unknowns), jnp.float32)]
        + [pltpu.SemaphoreType.DMA((7,)), pltpu.SemaphoreType.DMA((blocks,))],
        compiler_params=params,
        name="fill",
    )(*[pltpu.with_memory_space_constraint(whole, pltpu.HBM) for whole in inputs])
    arrived = [messages[0]] + [moved(messages[e], e) for e in range(1, LOW)]
    beside = [own_currents] + [moved(own_currents, d * LOW) for d in range(1, high_count)]
    box_lanes = -(-boxes // LANES) * LANES
    columns = f32((high_count * blocks, record, unknowns))
    half = LANES // 2
    tables = [
        pltpu.VMEM((half, 8, unknowns), jnp.float32),
        pltpu.VMEM((8, LANES), jnp.int32),
        pltpu.SMEM((8, LANES), jnp.int32),
        pltpu.SemaphoreType.DMA,
    ]
    first_sums = pl.pallas_call(
        functools.partial(sum_first_kernel, slots, high_count),
        out_shape=[columns, columns, f32((8, unknowns)), f32((8, box_lanes))],
        in_specs=[vmem] * (LOW // 2 + high_count),
        out_specs=[vmem] * 4,
        scratch_shapes=tables,
        compiler_params=params,
        name="sum_first",
    )(*arrived[: LOW // 2], *beside)
    partials = [f32((blocks * record + 8 * (1 + min(d // 2, 1)), unknowns)) for d in range(high_count)]
    everyone = ("basis", "pol")
    senders = basis_count * lax.axis_size("pol")
    *sums, grad = pl.pallas_call(
        functools.partial(sum_last_kernel, slots, high_count, blocks),
        out_shape=partials + [f32((senders, 1, box_lanes))],
        in_specs=[vmem] * (LOW // 2 + 4),
        out_specs=[vmem] * (high_count + 1),
        scratch_shapes=[pltpu.VMEM(columns.shape, jnp.float32)] + tables,
        compiler_params=params,
        name="sum_last",
    )(*arrived[LOW // 2 :], *first_sums)
    totals = [sums[0]] + [moved(sums[d], d * LOW) for d in range(1, high_count)]
    norm_far = 1.0 / math.sqrt(blocks * basis_count * unknowns)
    updated = pl.pallas_call(
        functools.partial(update_kernel, angles, norm_far, high_count),
        out_shape=f32(flat),
        in_specs=[vmem] * (high_count + 3),
        out_specs=vmem,
        compiler_params=params,
        name="update",
    )(*totals, adjoint_rows, radiation_rows, inverse)
    gathered = lax.all_to_all(grad, everyone, split_axis=0, concat_axis=0)
    gathered, updated = lax.optimization_barrier((gathered, updated))
    total_grad = jnp.sum(gathered[:, 0], axis=0)
    if lax.axis_size("angle") > 1:
        total_grad = lax.psum(total_grad, "angle")
    share = lax.dynamic_slice_in_dim(total_grad, lax.axis_index("basis") * BOX_DEV, BOX_DEV)
    shape_grad = share * (-1.0 / math.sqrt(4 * unknowns * angles_all * near_count))
    return (updated.reshape(adjoint.shape), shape_grad)


def solution(mesh):
    placed = (
        P("pol", "angle", "basis", None, None),
        P("pol", "angle", "basis", None, None),
        P("pol", "angle", "basis", None, None),
        P("basis", None, None, None, None),
        P("basis", None, None, None),
        P("basis", None),
        P("basis", None),
        P("basis"),
        P("basis", None),
    )
    return jax.shard_map(
        on_device,
        mesh=mesh,
        in_specs=placed,
        out_specs=(P("pol", "angle", "basis", None, None), P("basis")),
        check_vma=False,
    )
```

```python
import functools
import math

import jax
import jax.numpy as jnp
from jax import lax
from jax.experimental import pallas as pl
from jax.experimental.pallas import tpu as pltpu
from jax.sharding import PartitionSpec as P

LOW = 4
LANES = 128
BOX_DEV = 4
FAR_ROW = 3
VMEM_LIMIT = 48 * 1024 * 1024


def complex_rows(real, imag):
    return jnp.concatenate(
        [jnp.concatenate([real, imag], axis=1), jnp.concatenate([imag, -real], axis=1)], axis=0
    )


def fill_kernel(slots, *refs):
    whole_refs, message_refs, current_rows_ref = refs[:8], refs[8 : 8 + LOW], refs[8 + LOW]
    *held_refs, buffer_ref, sems, near_sems = refs[9 + LOW :]
    (
        col_device_ref,
        col_offset_ref,
        box_ref,
        rate_ref,
        adjoint_ref,
        currents_ref,
        radiation_ref,
        near_ref,
    ) = held_refs
    blocks, near_count = col_device_ref.shape
    stride = 2 * blocks
    angles = adjoint_ref.shape[0] // stride
    record = 2 * angles
    copies = [pltpu.make_async_copy(whole_refs[i], held_refs[i], sems.at[i]) for i in range(7)]
    near_copies = [
        pltpu.make_async_copy(
            whole_refs[7].at[pl.ds(row * near_count * 2, near_count * 2)],
            near_ref.at[pl.ds(row * near_count * 2, near_count * 2)],
            near_sems.at[row],
        )
        for row in range(blocks // 2)
    ]
    for copy in copies[4:5] + near_copies[:1] + copies[:4] + near_copies[1:] + copies[5:]:
        copy.start()
    me = lax.axis_index("basis")
    my_low = lax.rem(me, LOW)
    my_high = lax.div(me, LOW)
    spread = LANES // LOW
    lane8 = lax.broadcasted_iota(jnp.int32, (8, LANES), 1)
    sub8 = lax.broadcasted_iota(jnp.int32, (8, LANES), 0)
    table = jnp.zeros((8, LANES), jnp.float32)
    counts = [jnp.int32(0)] * LOW
    buffer_ref[...] = jnp.zeros(buffer_ref.shape, jnp.float32)
    for copy in copies[:5]:
        copy.wait()
    for row in range(blocks):
        real = adjoint_ref[pl.ds(2 * row, angles, stride=stride), :].astype(jnp.bfloat16)
        imag = adjoint_ref[pl.ds(2 * row + 1, angles, stride=stride), :].astype(jnp.bfloat16)
        left = complex_rows(real, imag)
        box = box_ref[row].astype(jnp.float32)
        if row % 2 == 0:
            near_copies[row // 2].wait()
        for first in range(0, near_count, 1):
            some = range(first, min(first + 1, near_count))
            right = jnp.concatenate([near_ref[row * near_count + k] for k in some], axis=1)
            terms = jnp.dot(left, right, preferred_element_type=jnp.float32)
            for k in some:
                device = col_device_ref[row, k]
                low = lax.bitwise_xor(lax.rem(device, LOW), my_low)
                high = lax.bitwise_xor(lax.div(device, LOW), my_high)
                place = high * blocks + col_offset_ref[row, k]
                slot = jnp.int32(0)
                for e in range(LOW):
                    here = low == e
                    slot = jnp.where(here, counts[e], slot)
                    counts[e] = counts[e] + here.astype(jnp.int32)
                slot = jnp.minimum(slot, slots - 1)
                buffer_ref[low * slots + slot] = terms[:, (k - first) * LANES : (k - first + 1) * LANES]
                entry = jnp.where(
                    sub8 == 0, place.astype(jnp.float32), jnp.where(sub8 == 1, rate_ref[row, k], box)
                )
                table = jnp.where(lane8 == low * spread + slot, entry, table)
    for copy in copies[5:]:
        copy.wait()
    for row in range(blocks):
        for part in range(2):
            current_rows_ref[row, pl.ds(part * angles, angles), :] = currents_ref[
                pl.ds(2 * row + part, angles, stride=stride), :
            ]
    count = angles * blocks
    rad_real = radiation_ref[pl.ds(0, count, stride=2), :]
    rad_imag = radiation_ref[pl.ds(1, count, stride=2), :]
    cur_real = currents_ref[pl.ds(0, count, stride=2), :]
    cur_imag = currents_ref[pl.ds(1, count, stride=2), :]
    far_real = jnp.sum((rad_real * cur_real - rad_imag * cur_imag).reshape(angles, blocks, LANES), axis=1)
    far_imag = jnp.sum((rad_real * cur_imag + rad_imag * cur_real).reshape(angles, blocks, LANES), axis=1)
    lane = lax.broadcasted_iota(jnp.int32, (angles, LANES), 1)
    angle = lax.broadcasted_iota(jnp.int32, (angles, LANES), 0)
    far = jnp.where(lane == angle, jnp.sum(far_real, axis=1, keepdims=True), 0.0) + jnp.where(
        lane == angle + angles, jnp.sum(far_imag, axis=1, keepdims=True), 0.0
    )
    far = jnp.broadcast_to(jnp.sum(far, axis=0, keepdims=True), (8, LANES))
    for e in range(LOW):
        for s in range(slots):
            message_refs[e][pl.ds(s * record, record), :] = buffer_ref[e * slots + s]
        mine = jnp.where(lane8 // spread == e, table, 0.0)
        message_refs[e][pl.ds(slots * record, 8), :] = jnp.where(sub8 == FAR_ROW, far, mine)


def add_slots(message_refs, first, slots, boxes, table, scratch_refs):
    acc_ref, cur_ref, prod_ref, table_ref, place_ref, sem = scratch_refs
    spread = LANES // LOW
    record = cur_ref.shape[1]
    table_ref[...] = table.astype(jnp.int32)
    copy = pltpu.make_async_copy(table_ref, place_ref, sem)
    copy.start()
    prod_ref[...] = jnp.zeros(prod_ref.shape, jnp.float32)
    count = len(message_refs) * spread
    by_pair = jnp.transpose(table)[first * spread : first * spread + count]
    number = lax.broadcasted_iota(jnp.int32, (count, boxes), 1).astype(jnp.float32)
    rates = jnp.where(by_pair[:, 2:3] == number, by_pair[:, 1:2], 0.0)
    copy.wait()
    for i, message_ref in enumerate(message_refs):
        for s in range(slots):
            at = place_ref[0, (first + i) * spread + s]
            term = message_ref[pl.ds(s * record, record), :]
            acc_ref[at] = acc_ref[at] + term
            both = term * cur_ref[at]
            prod_ref[i * spread + s] = jnp.sum(both.reshape(-1, 8, LANES), axis=0)
    by_slot = jnp.sum(jnp.sum(prod_ref[...], axis=1), axis=1, keepdims=True)
    return jnp.sum((rates * by_slot).reshape(count // 8, 8, boxes), axis=0)


def sum_first_kernel(slots, high_count, *refs):
    message_refs, current_refs = refs[: LOW // 2], refs[LOW // 2 : LOW // 2 + high_count]
    acc_ref, cur_ref, extra_ref, share_ref, *scratch_refs = refs[LOW // 2 + high_count :]
    blocks, record = current_refs[0].shape[:2]
    extra = functools.reduce(jnp.add, [ref[pl.ds(slots * record, 8), :] for ref in message_refs])
    for d in range(high_count):
        cur_ref[pl.ds(d * blocks, blocks)] = current_refs[d][...]
    acc_ref[...] = jnp.zeros(acc_ref.shape, jnp.float32)
    share_ref[...] = add_slots(message_refs, 0, slots, share_ref.shape[1], extra, (acc_ref, cur_ref, *scratch_refs))
    extra_ref[...] = extra


def sum_last_kernel(slots, high_count, blocks, *refs):
    message_refs, refs = refs[: LOW // 2], refs[LOW // 2 :]
    (first_ref, cur_ref, first_extra_ref, first_share_ref), refs = refs[:4], refs[4:]
    out_refs, (grad_ref, acc_ref, *scratch_refs) = refs[:high_count], refs[high_count:]
    record = cur_ref.shape[1]
    extra = functools.reduce(jnp.add, [ref[pl.ds(slots * record, 8), :] for ref in message_refs])
    acc_ref[...] = first_ref[...]
    share = add_slots(message_refs, LOW // 2, slots, grad_ref.shape[2], extra, (acc_ref, cur_ref, *scratch_refs))
    box_sums = jnp.sum(share + first_share_ref[...], axis=0, keepdims=True)
    grad_ref[...] = jnp.broadcast_to(box_sums[None], grad_ref.shape)
    extra = extra + first_extra_ref[...]
    for d in range(high_count):
        for b in range(blocks):
            out_refs[d][pl.ds(b * record, record), :] = acc_ref[d * blocks + b]
        for row in range(blocks * record, out_refs[d].shape[0], 8):
            out_refs[d][pl.ds(row, 8), :] = extra


def update_kernel(angles, norm_far, high_count, *refs):
    sum_refs = refs[:high_count]
    adjoint_ref, radiation_ref, inverse_ref, out_ref = refs[high_count:]
    blocks = inverse_ref.shape[0]
    stride = 2 * blocks
    record = 2 * angles

    def total(start, rows):
        return functools.reduce(jnp.add, [ref[pl.ds(start, rows), :] for ref in sum_refs])

    far = total(blocks * record, 8)[FAR_ROW : FAR_ROW + 1] * norm_far
    lane = lax.broadcasted_iota(jnp.int32, (angles, LANES), 1)
    angle = lax.broadcasted_iota(jnp.int32, (angles, LANES), 0)
    far_real = jnp.sum(jnp.where(lane == angle, far, 0.0), axis=1, keepdims=True)
    far_imag = jnp.sum(jnp.where(lane == angle + angles, far, 0.0), axis=1, keepdims=True)
    far_real = jnp.broadcast_to(far_real, (angles, LANES))
    far_imag = jnp.broadcast_to(far_imag, (angles, LANES))
    for block in range(blocks):
        rows_real = pl.ds(2 * block, angles, stride=stride)
        rows_imag = pl.ds(2 * block + 1, angles, stride=stride)
        near = total(block * record, record)
        rad_real, rad_imag = radiation_ref[rows_real, :], radiation_ref[rows_imag, :]
        real = (far_real * rad_real + far_imag * rad_imag - near[:angles]).astype(jnp.bfloat16)
        imag = (far_imag * rad_real - far_real * rad_imag - near[angles:]).astype(jnp.bfloat16)
        step = jnp.dot(complex_rows(real, imag), inverse_ref[block], preferred_element_type=jnp.float32)
        out_ref[rows_real, :] = adjoint_ref[rows_real, :] + step[:angles]
        out_ref[rows_imag, :] = adjoint_ref[rows_imag, :] + step[angles:]


def on_device(
    adjoint,
    currents,
    radiation,
    near_blocks,
    inverse_blocks,
    col_device,
    col_offset,
    box_of_block,
    pair_rate,
):
    angles, blocks, unknowns = adjoint.shape[1], adjoint.shape[2], adjoint.shape[4]
    near_count = near_blocks.shape[1]
    pairs = blocks * near_count
    record = 2 * angles
    basis_count = lax.axis_size("basis")
    high_count = basis_count // LOW
    angles_all = angles * lax.axis_size("angle")
    boxes = BOX_DEV * basis_count
    slots = 2 * pairs // basis_count * high_count
    vmem = pl.BlockSpec(memory_space=pltpu.VMEM)
    params = pltpu.CompilerParams(vmem_limit_bytes=VMEM_LIMIT)

    def moved(value, bits):
        return lax.ppermute(value, "basis", [(i, i ^ bits) for i in range(basis_count)])

    flat = (angles * blocks * 2, unknowns)
    adjoint_rows = adjoint.reshape(flat)
    currents_rows = currents.reshape(flat)
    radiation_rows = radiation.reshape(flat)
    near = near_blocks.reshape(pairs, 2 * unknowns, unknowns)
    inverse = inverse_blocks.reshape(blocks, 2 * unknowns, unknowns)
    f32 = functools.partial(jax.ShapeDtypeStruct, dtype=jnp.float32)
    message = f32((slots * record + 8, unknowns))
    inputs = (
        col_device,
        col_offset,
        box_of_block,
        pair_rate,
        adjoint_rows,
        currents_rows,
        radiation_rows,
        near,
    )
    *messages, own_currents = pl.pallas_call(
        functools.partial(fill_kernel, slots),
        out_shape=[message] * LOW + [f32((blocks, record, unknowns))],
        in_specs=[pl.BlockSpec(memory_space=pltpu.HBM)] * len(inputs),
        out_specs=[vmem] * (LOW + 1),
        scratch_shapes=[pltpu.SMEM(whole.shape, whole.dtype) for whole in inputs[:4]]
        + [pltpu.VMEM(whole.shape, whole.dtype) for whole in inputs[4:]]
        + [pltpu.VMEM((LOW * slots, record, unknowns), jnp.float32)]
        + [pltpu.SemaphoreType.DMA((7,)), pltpu.SemaphoreType.DMA((blocks,))],
        compiler_params=params,
        name="fill",
    )(*[pltpu.with_memory_space_constraint(whole, pltpu.HBM) for whole in inputs])
    arrived = [messages[0]] + [moved(messages[e], e) for e in range(1, LOW)]
    beside = [own_currents] + [moved(own_currents, d * LOW) for d in range(1, high_count)]
    box_lanes = -(-boxes // LANES) * LANES
    columns = f32((high_count * blocks, record, unknowns))
    half = LANES // 2
    tables = [
        pltpu.VMEM((half, 8, unknowns), jnp.float32),
        pltpu.VMEM((8, LANES), jnp.int32),
        pltpu.SMEM((8, LANES), jnp.int32),
        pltpu.SemaphoreType.DMA,
    ]
    first_sums = pl.pallas_call(
        functools.partial(sum_first_kernel, slots, high_count),
        out_shape=[columns, columns, f32((8, unknowns)), f32((8, box_lanes))],
        in_specs=[vmem] * (LOW // 2 + high_count),
        out_specs=[vmem] * 4,
        scratch_shapes=tables,
        compiler_params=params,
        name="sum_first",
    )(*arrived[: LOW // 2], *beside)
    partials = [f32((blocks * record + 8 * (1 + min(d // 2, 1)), unknowns)) for d in range(high_count)]
    everyone = ("basis", "pol")
    senders = basis_count * lax.axis_size("pol")
    *sums, grad = pl.pallas_call(
        functools.partial(sum_last_kernel, slots, high_count, blocks),
        out_shape=partials + [f32((senders, 1, box_lanes))],
        in_specs=[vmem] * (LOW // 2 + 4),
        out_specs=[vmem] * (high_count + 1),
        scratch_shapes=[pltpu.VMEM(columns.shape, jnp.float32)] + tables,
        compiler_params=params,
        name="sum_last",
    )(*arrived[LOW // 2 :], *first_sums)
    totals = [sums[0]] + [moved(sums[d], d * LOW) for d in range(1, high_count)]
    norm_far = 1.0 / math.sqrt(blocks * basis_count * unknowns)
    updated = pl.pallas_call(
        functools.partial(update_kernel, angles, norm_far, high_count),
        out_shape=f32(flat),
        in_specs=[vmem] * (high_count + 3),
        out_specs=vmem,
        compiler_params=params,
        name="update",
    )(*totals, adjoint_rows, radiation_rows, inverse)
    gathered = lax.all_to_all(grad, everyone, split_axis=0, concat_axis=0)
    gathered, updated = lax.optimization_barrier((gathered, updated))
    total_grad = jnp.sum(gathered[:, 0], axis=0)
    if lax.axis_size("angle") > 1:
        total_grad = lax.psum(total_grad, "angle")
    share = lax.dynamic_slice_in_dim(total_grad, lax.axis_index("basis") * BOX_DEV, BOX_DEV)
    shape_grad = share * (-1.0 / math.sqrt(4 * unknowns * angles_all * near_count))
    return (updated.reshape(adjoint.shape), shape_grad)


def solution(mesh):
    placed = (
        P("pol", "angle", "basis", None, None),
        P("pol", "angle", "basis", None, None),
        P("pol", "angle", "basis", None, None),
        P("basis", None, None, None, None),
        P("basis", None, None, None),
        P("basis", None),
        P("basis", None),
        P("basis"),
        P("basis", None),
    )
    return jax.shard_map(
        on_device,
        mesh=mesh,
        in_specs=placed,
        out_specs=(P("pol", "angle", "basis", None, None), P("basis")),
        check_vma=False,
    )
```

```python
import functools
import math

import jax
import jax.numpy as jnp
from jax import lax
from jax.experimental import pallas as pl
from jax.experimental.pallas import tpu as pltpu
from jax.sharding import PartitionSpec as P

LOW = 4
LANES = 128
BOX_DEV = 4
FAR_ROW = 3
VMEM_LIMIT = 48 * 1024 * 1024


def complex_rows(real, imag):
    return jnp.concatenate(
        [jnp.concatenate([real, imag], axis=1), jnp.concatenate([imag, -real], axis=1)], axis=0
    )


def fill_kernel(slots, *refs):
    whole_refs, message_refs, current_rows_ref = refs[:8], refs[8 : 8 + LOW], refs[8 + LOW]
    *held_refs, buffer_ref, sems, near_sems = refs[9 + LOW :]
    (
        col_device_ref,
        col_offset_ref,
        box_ref,
        rate_ref,
        adjoint_ref,
        currents_ref,
        radiation_ref,
        near_ref,
    ) = held_refs
    blocks, near_count = col_device_ref.shape
    stride = 2 * blocks
    angles = adjoint_ref.shape[0] // stride
    record = 2 * angles
    copies = [pltpu.make_async_copy(whole_refs[i], held_refs[i], sems.at[i]) for i in range(7)]
    near_copies = [
        pltpu.make_async_copy(
            whole_refs[7].at[pl.ds(row * near_count * 2, near_count * 2)],
            near_ref.at[pl.ds(row * near_count * 2, near_count * 2)],
            near_sems.at[row],
        )
        for row in range(blocks // 2)
    ]
    for copy in copies[4:5] + near_copies[:1] + copies[:4] + near_copies[1:] + copies[5:]:
        copy.start()
    me = lax.axis_index("basis")
    my_low = lax.rem(me, LOW)
    my_high = lax.div(me, LOW)
    spread = LANES // LOW
    lane8 = lax.broadcasted_iota(jnp.int32, (8, LANES), 1)
    sub8 = lax.broadcasted_iota(jnp.int32, (8, LANES), 0)
    table = jnp.zeros((8, LANES), jnp.float32)
    counts = [jnp.int32(0)] * LOW
    buffer_ref[...] = jnp.zeros(buffer_ref.shape, jnp.float32)
    for copy in copies[:5]:
        copy.wait()
    for row in range(blocks):
        real = adjoint_ref[pl.ds(2 * row, angles, stride=stride), :].astype(jnp.bfloat16)
        imag = adjoint_ref[pl.ds(2 * row + 1, angles, stride=stride), :].astype(jnp.bfloat16)
        left = complex_rows(real, imag)
        box = box_ref[row].astype(jnp.float32)
        if row % 2 == 0:
            near_copies[row // 2].wait()
        for first in range(0, near_count, 1):
            some = range(first, min(first + 1, near_count))
            right = jnp.concatenate([near_ref[row * near_count + k] for k in some], axis=1)
            terms = jnp.dot(left, right, preferred_element_type=jnp.float32)
            for k in some:
                device = col_device_ref[row, k]
                low = lax.bitwise_xor(lax.rem(device, LOW), my_low)
                high = lax.bitwise_xor(lax.div(device, LOW), my_high)
                place = high * blocks + col_offset_ref[row, k]
                slot = jnp.int32(0)
                for e in range(LOW):
                    here = low == e
                    slot = jnp.where(here, counts[e], slot)
                    counts[e] = counts[e] + here.astype(jnp.int32)
                slot = jnp.minimum(slot, slots - 1)
                buffer_ref[low * slots + slot] = terms[:, (k - first) * LANES : (k - first + 1) * LANES]
                entry = jnp.where(
                    sub8 == 0, place.astype(jnp.float32), jnp.where(sub8 == 1, rate_ref[row, k], box)
                )
                table = jnp.where(lane8 == low * spread + slot, entry, table)
    for copy in copies[5:]:
        copy.wait()
    for row in range(blocks):
        for part in range(2):
            current_rows_ref[row, pl.ds(part * angles, angles), :] = currents_ref[
                pl.ds(2 * row + part, angles, stride=stride), :
            ]
    count = angles * blocks
    rad_real = radiation_ref[pl.ds(0, count, stride=2), :]
    rad_imag = radiation_ref[pl.ds(1, count, stride=2), :]
    cur_real = currents_ref[pl.ds(0, count, stride=2), :]
    cur_imag = currents_ref[pl.ds(1, count, stride=2), :]
    far_real = jnp.sum((rad_real * cur_real - rad_imag * cur_imag).reshape(angles, blocks, LANES), axis=1)
    far_imag = jnp.sum((rad_real * cur_imag + rad_imag * cur_real).reshape(angles, blocks, LANES), axis=1)
    lane = lax.broadcasted_iota(jnp.int32, (angles, LANES), 1)
    angle = lax.broadcasted_iota(jnp.int32, (angles, LANES), 0)
    far = jnp.where(lane == angle, jnp.sum(far_real, axis=1, keepdims=True), 0.0) + jnp.where(
        lane == angle + angles, jnp.sum(far_imag, axis=1, keepdims=True), 0.0
    )
    far = jnp.broadcast_to(jnp.sum(far, axis=0, keepdims=True), (8, LANES))
    for e in range(LOW):
        for s in range(slots):
            message_refs[e][pl.ds(s * record, record), :] = buffer_ref[e * slots + s]
        mine = jnp.where(lane8 // spread == e, table, 0.0)
        message_refs[e][pl.ds(slots * record, 8), :] = jnp.where(sub8 == FAR_ROW, far, mine)


def start_places(table, table_ref, place_ref, sem):
    table_ref[...] = table.astype(jnp.int32)
    copy = pltpu.make_async_copy(table_ref, place_ref, sem)
    copy.start()
    return copy


def box_shares(message_refs, first, slots, boxes, table, cur_ref, prod_ref, place_ref, copy):
    spread = LANES // LOW
    record = cur_ref.shape[1]
    prod_ref[...] = jnp.zeros(prod_ref.shape, jnp.float32)
    count = len(message_refs) * spread
    by_pair = jnp.transpose(table)[first * spread : first * spread + count]
    number = lax.broadcasted_iota(jnp.int32, (count, boxes), 1).astype(jnp.float32)
    rates = jnp.where(by_pair[:, 2:3] == number, by_pair[:, 1:2], 0.0)
    copy.wait()
    for i, message_ref in enumerate(message_refs):
        for s in range(slots):
            at = place_ref[0, (first + i) * spread + s]
            both = message_ref[pl.ds(s * record, record), :] * cur_ref[at]
            prod_ref[i * spread + s] = jnp.sum(both.reshape(-1, 8, LANES), axis=0)
    by_slot = jnp.sum(jnp.sum(prod_ref[...], axis=1), axis=1, keepdims=True)
    return jnp.sum((rates * by_slot).reshape(count // 8, 8, boxes), axis=0)


def add_slots(message_refs, first, slots, record, acc_ref, place_ref):
    for i, message_ref in enumerate(message_refs):
        for s in range(slots):
            at = place_ref[0, (first + i) * (LANES // LOW) + s]
            acc_ref[at] = acc_ref[at] + message_ref[pl.ds(s * record, record), :]


def sum_first_kernel(slots, high_count, *refs):
    message_refs, current_refs = refs[: LOW // 2], refs[LOW // 2 : LOW // 2 + high_count]
    acc_ref, cur_ref, extra_ref, share_ref, prod_ref, table_ref, place_ref, sem = refs[
        LOW // 2 + high_count :
    ]
    blocks, record = current_refs[0].shape[:2]
    extra = functools.reduce(jnp.add, [ref[pl.ds(slots * record, 8), :] for ref in message_refs])
    copy = start_places(extra, table_ref, place_ref, sem)
    for d in range(high_count):
        cur_ref[pl.ds(d * blocks, blocks)] = current_refs[d][...]
    acc_ref[...] = jnp.zeros(acc_ref.shape, jnp.float32)
    share_ref[...] = box_shares(
        message_refs, 0, slots, share_ref.shape[1], extra, cur_ref, prod_ref, place_ref, copy
    )
    add_slots(message_refs, 0, slots, record, acc_ref, place_ref)
    extra_ref[...] = extra


def sum_last_kernel(slots, high_count, blocks, *refs):
    message_refs, refs = refs[: LOW // 2], refs[LOW // 2 :]
    (first_ref, cur_ref, first_extra_ref, first_share_ref), refs = refs[:4], refs[4:]
    out_refs, (whole_grad_ref, acc_ref, *refs) = refs[:high_count], refs[high_count:]
    prod_ref, table_ref, place_ref, sem, grad_ref, grad_sem = refs
    record = cur_ref.shape[1]
    extra = functools.reduce(jnp.add, [ref[pl.ds(slots * record, 8), :] for ref in message_refs])
    copy = start_places(extra, table_ref, place_ref, sem)
    acc_ref[...] = first_ref[...]
    share = box_shares(
        message_refs, LOW // 2, slots, grad_ref.shape[2], extra, cur_ref, prod_ref, place_ref, copy
    )
    box_sums = jnp.sum(share + first_share_ref[...], axis=0, keepdims=True)
    grad_ref[...] = jnp.broadcast_to(box_sums[None], grad_ref.shape)
    copy = pltpu.make_async_copy(grad_ref, whole_grad_ref, grad_sem)
    copy.start()
    add_slots(message_refs, LOW // 2, slots, record, acc_ref, place_ref)
    extra = extra + first_extra_ref[...]
    for d in range(high_count):
        for b in range(blocks):
            out_refs[d][pl.ds(b * record, record), :] = acc_ref[d * blocks + b]
        for row in range(blocks * record, out_refs[d].shape[0], 8):
            out_refs[d][pl.ds(row, 8), :] = extra
    copy.wait()


def update_kernel(angles, norm_far, high_count, *refs):
    sum_refs = refs[:high_count]
    adjoint_ref, radiation_ref, inverse_ref, out_ref = refs[high_count:]
    blocks = inverse_ref.shape[0]
    stride = 2 * blocks
    record = 2 * angles

    def total(start, rows):
        return functools.reduce(jnp.add, [ref[pl.ds(start, rows), :] for ref in sum_refs])

    far = total(blocks * record, 8)[FAR_ROW : FAR_ROW + 1] * norm_far
    lane = lax.broadcasted_iota(jnp.int32, (angles, LANES), 1)
    angle = lax.broadcasted_iota(jnp.int32, (angles, LANES), 0)
    far_real = jnp.sum(jnp.where(lane == angle, far, 0.0), axis=1, keepdims=True)
    far_imag = jnp.sum(jnp.where(lane == angle + angles, far, 0.0), axis=1, keepdims=True)
    far_real = jnp.broadcast_to(far_real, (angles, LANES))
    far_imag = jnp.broadcast_to(far_imag, (angles, LANES))
    for block in range(blocks):
        rows_real = pl.ds(2 * block, angles, stride=stride)
        rows_imag = pl.ds(2 * block + 1, angles, stride=stride)
        near = total(block * record, record)
        rad_real, rad_imag = radiation_ref[rows_real, :], radiation_ref[rows_imag, :]
        real = (far_real * rad_real + far_imag * rad_imag - near[:angles]).astype(jnp.bfloat16)
        imag = (far_imag * rad_real - far_real * rad_imag - near[angles:]).astype(jnp.bfloat16)
        step = jnp.dot(complex_rows(real, imag), inverse_ref[block], preferred_element_type=jnp.float32)
        out_ref[rows_real, :] = adjoint_ref[rows_real, :] + step[:angles]
        out_ref[rows_imag, :] = adjoint_ref[rows_imag, :] + step[angles:]


def on_device(
    adjoint,
    currents,
    radiation,
    near_blocks,
    inverse_blocks,
    col_device,
    col_offset,
    box_of_block,
    pair_rate,
):
    angles, blocks, unknowns = adjoint.shape[1], adjoint.shape[2], adjoint.shape[4]
    near_count = near_blocks.shape[1]
    pairs = blocks * near_count
    record = 2 * angles
    basis_count = lax.axis_size("basis")
    high_count = basis_count // LOW
    angles_all = angles * lax.axis_size("angle")
    boxes = BOX_DEV * basis_count
    slots = 2 * pairs // basis_count * high_count
    vmem = pl.BlockSpec(memory_space=pltpu.VMEM)
    params = pltpu.CompilerParams(vmem_limit_bytes=VMEM_LIMIT)

    def moved(value, bits):
        return lax.ppermute(value, "basis", [(i, i ^ bits) for i in range(basis_count)])

    flat = (angles * blocks * 2, unknowns)
    adjoint_rows = adjoint.reshape(flat)
    currents_rows = currents.reshape(flat)
    radiation_rows = radiation.reshape(flat)
    near = near_blocks.reshape(pairs, 2 * unknowns, unknowns)
    inverse = inverse_blocks.reshape(blocks, 2 * unknowns, unknowns)
    f32 = functools.partial(jax.ShapeDtypeStruct, dtype=jnp.float32)
    message = f32((slots * record + 8, unknowns))
    inputs = (
        col_device,
        col_offset,
        box_of_block,
        pair_rate,
        adjoint_rows,
        currents_rows,
        radiation_rows,
        near,
    )
    *messages, own_currents = pl.pallas_call(
        functools.partial(fill_kernel, slots),
        out_shape=[message] * LOW + [f32((blocks, record, unknowns))],
        in_specs=[pl.BlockSpec(memory_space=pltpu.HBM)] * len(inputs),
        out_specs=[vmem] * (LOW + 1),
        scratch_shapes=[pltpu.SMEM(whole.shape, whole.dtype) for whole in inputs[:4]]
        + [pltpu.VMEM(whole.shape, whole.dtype) for whole in inputs[4:]]
        + [pltpu.VMEM((LOW * slots, record, unknowns), jnp.float32)]
        + [pltpu.SemaphoreType.DMA((7,)), pltpu.SemaphoreType.DMA((blocks,))],
        compiler_params=params,
        name="fill",
    )(*[pltpu.with_memory_space_constraint(whole, pltpu.HBM) for whole in inputs])
    arrived = [messages[0]] + [moved(messages[e], e) for e in range(1, LOW)]
    beside = [own_currents] + [moved(own_currents, d * LOW) for d in range(1, high_count)]
    box_lanes = -(-boxes // LANES) * LANES
    columns = f32((high_count * blocks, record, unknowns))
    half = LANES // 2
    tables = [
        pltpu.VMEM((half, 8, unknowns), jnp.float32),
        pltpu.VMEM((8, LANES), jnp.int32),
        pltpu.SMEM((8, LANES), jnp.int32),
        pltpu.SemaphoreType.DMA,
    ]
    first_sums = pl.pallas_call(
        functools.partial(sum_first_kernel, slots, high_count),
        out_shape=[columns, columns, f32((8, unknowns)), f32((8, box_lanes))],
        in_specs=[vmem] * (LOW // 2 + high_count),
        out_specs=[vmem] * 4,
        scratch_shapes=tables,
        compiler_params=params,
        name="sum_first",
    )(*arrived[: LOW // 2], *beside)
    partials = [f32((blocks * record + 8 * (1 + min(d // 2, 1)), unknowns)) for d in range(high_count)]
    everyone = ("basis", "pol")
    senders = basis_count * lax.axis_size("pol")
    *sums, grad = pl.pallas_call(
        functools.partial(sum_last_kernel, slots, high_count, blocks),
        out_shape=partials + [f32((senders, 1, box_lanes))],
        in_specs=[vmem] * (LOW // 2 + 4),
        out_specs=[vmem] * high_count + [pl.BlockSpec(memory_space=pltpu.HBM)],
        scratch_shapes=[pltpu.VMEM(columns.shape, jnp.float32)]
        + tables
        + [pltpu.VMEM((senders, 1, box_lanes), jnp.float32), pltpu.SemaphoreType.DMA],
        compiler_params=params,
        name="sum_last",
    )(*arrived[LOW // 2 :], *first_sums)
    totals = [sums[0]] + [moved(sums[d], d * LOW) for d in range(1, high_count)]
    norm_far = 1.0 / math.sqrt(blocks * basis_count * unknowns)
    updated = pl.pallas_call(
        functools.partial(update_kernel, angles, norm_far, high_count),
        out_shape=f32(flat),
        in_specs=[vmem] * (high_count + 3),
        out_specs=vmem,
        compiler_params=params,
        name="update",
    )(*totals, adjoint_rows, radiation_rows, inverse)
    gathered = lax.all_to_all(grad, everyone, split_axis=0, concat_axis=0)
    gathered, updated = lax.optimization_barrier((gathered, updated))
    total_grad = jnp.sum(gathered[:, 0], axis=0)
    if lax.axis_size("angle") > 1:
        total_grad = lax.psum(total_grad, "angle")
    share = lax.dynamic_slice_in_dim(total_grad, lax.axis_index("basis") * BOX_DEV, BOX_DEV)
    shape_grad = share * (-1.0 / math.sqrt(4 * unknowns * angles_all * near_count))
    return (updated.reshape(adjoint.shape), shape_grad)


def solution(mesh):
    placed = (
        P("pol", "angle", "basis", None, None),
        P("pol", "angle", "basis", None, None),
        P("pol", "angle", "basis", None, None),
        P("basis", None, None, None, None),
        P("basis", None, None, None),
        P("basis", None),
        P("basis", None),
        P("basis"),
        P("basis", None),
    )
    return jax.shard_map(
        on_device,
        mesh=mesh,
        in_specs=placed,
        out_specs=(P("pol", "angle", "basis", None, None), P("basis")),
        check_vma=False,
    )
```

```python
import functools
import math

import jax
import jax.numpy as jnp
from jax import lax
from jax.experimental import pallas as pl
from jax.experimental.pallas import tpu as pltpu
from jax.sharding import PartitionSpec as P

LOW = 4
LANES = 128
BOX_DEV = 4
FAR_ROW = 3
VMEM_LIMIT = 48 * 1024 * 1024


def complex_rows(real, imag):
    return jnp.concatenate(
        [jnp.concatenate([real, imag], axis=1), jnp.concatenate([imag, -real], axis=1)], axis=0
    )


def fill_kernel(slots, *refs):
    whole_refs, message_refs, current_rows_ref = refs[:8], refs[8 : 8 + LOW], refs[8 + LOW]
    *held_refs, buffer_ref, sems, near_sems = refs[9 + LOW :]
    (
        col_device_ref,
        col_offset_ref,
        box_ref,
        rate_ref,
        adjoint_ref,
        currents_ref,
        radiation_ref,
        near_ref,
    ) = held_refs
    blocks, near_count = col_device_ref.shape
    stride = 2 * blocks
    angles = adjoint_ref.shape[0] // stride
    record = 2 * angles
    copies = [pltpu.make_async_copy(whole_refs[i], held_refs[i], sems.at[i]) for i in range(7)]
    near_copies = [
        pltpu.make_async_copy(
            whole_refs[7].at[pl.ds(row * near_count * 2, near_count * 2)],
            near_ref.at[pl.ds(row * near_count * 2, near_count * 2)],
            near_sems.at[row],
        )
        for row in range(blocks // 2)
    ]
    for copy in copies[4:5] + near_copies[:1] + copies[:4] + near_copies[1:] + copies[5:]:
        copy.start()
    me = lax.axis_index("basis")
    my_low = lax.rem(me, LOW)
    my_high = lax.div(me, LOW)
    spread = LANES // LOW
    lane8 = lax.broadcasted_iota(jnp.int32, (8, LANES), 1)
    sub8 = lax.broadcasted_iota(jnp.int32, (8, LANES), 0)
    table = jnp.zeros((8, LANES), jnp.float32)
    counts = [jnp.int32(0)] * LOW
    buffer_ref[...] = jnp.zeros(buffer_ref.shape, jnp.float32)
    for copy in copies[:5]:
        copy.wait()
    for row in range(blocks):
        real = adjoint_ref[pl.ds(2 * row, angles, stride=stride), :].astype(jnp.bfloat16)
        imag = adjoint_ref[pl.ds(2 * row + 1, angles, stride=stride), :].astype(jnp.bfloat16)
        left = complex_rows(real, imag)
        box = box_ref[row].astype(jnp.float32)
        if row % 2 == 0:
            near_copies[row // 2].wait()
        for first in range(0, near_count, 1):
            some = range(first, min(first + 1, near_count))
            right = jnp.concatenate([near_ref[row * near_count + k] for k in some], axis=1)
            terms = jnp.dot(left, right, preferred_element_type=jnp.float32)
            for k in some:
                device = col_device_ref[row, k]
                low = lax.bitwise_xor(lax.rem(device, LOW), my_low)
                high = lax.bitwise_xor(lax.div(device, LOW), my_high)
                place = high * blocks + col_offset_ref[row, k]
                slot = jnp.int32(0)
                for e in range(LOW):
                    here = low == e
                    slot = jnp.where(here, counts[e], slot)
                    counts[e] = counts[e] + here.astype(jnp.int32)
                slot = jnp.minimum(slot, slots - 1)
                buffer_ref[low * slots + slot] = terms[:, (k - first) * LANES : (k - first + 1) * LANES]
                entry = jnp.where(
                    sub8 == 0, place.astype(jnp.float32), jnp.where(sub8 == 1, rate_ref[row, k], box)
                )
                table = jnp.where(lane8 == low * spread + slot, entry, table)
    for copy in copies[5:]:
        copy.wait()
    for row in range(blocks):
        for part in range(2):
            current_rows_ref[row, pl.ds(part * angles, angles), :] = currents_ref[
                pl.ds(2 * row + part, angles, stride=stride), :
            ]
    count = angles * blocks
    rad_real = radiation_ref[pl.ds(0, count, stride=2), :]
    rad_imag = radiation_ref[pl.ds(1, count, stride=2), :]
    cur_real = currents_ref[pl.ds(0, count, stride=2), :]
    cur_imag = currents_ref[pl.ds(1, count, stride=2), :]
    far_real = jnp.sum((rad_real * cur_real - rad_imag * cur_imag).reshape(angles, blocks, LANES), axis=1)
    far_imag = jnp.sum((rad_real * cur_imag + rad_imag * cur_real).reshape(angles, blocks, LANES), axis=1)
    lane = lax.broadcasted_iota(jnp.int32, (angles, LANES), 1)
    angle = lax.broadcasted_iota(jnp.int32, (angles, LANES), 0)
    far = jnp.where(lane == angle, jnp.sum(far_real, axis=1, keepdims=True), 0.0) + jnp.where(
        lane == angle + angles, jnp.sum(far_imag, axis=1, keepdims=True), 0.0
    )
    far = jnp.broadcast_to(jnp.sum(far, axis=0, keepdims=True), (8, LANES))
    for e in range(LOW):
        for s in range(slots):
            message_refs[e][pl.ds(s * record, record), :] = buffer_ref[e * slots + s]
        mine = jnp.where(lane8 // spread == e, table, 0.0)
        message_refs[e][pl.ds(slots * record, 8), :] = jnp.where(sub8 == FAR_ROW, far, mine)


def start_places(table, table_ref, place_ref, sem):
    table_ref[...] = table.astype(jnp.int32)
    copy = pltpu.make_async_copy(table_ref, place_ref, sem)
    copy.start()
    return copy


def box_shares(message_refs, first, slots, boxes, table, cur_ref, prod_ref, place_ref, copy):
    spread = LANES // LOW
    record = cur_ref.shape[1]
    prod_ref[...] = jnp.zeros(prod_ref.shape, jnp.float32)
    count = len(message_refs) * spread
    by_pair = jnp.transpose(table)[first * spread : first * spread + count]
    number = lax.broadcasted_iota(jnp.int32, (count, boxes), 1).astype(jnp.float32)
    rates = jnp.where(by_pair[:, 2:3] == number, by_pair[:, 1:2], 0.0)
    copy.wait()
    for i, message_ref in enumerate(message_refs):
        for s in range(slots):
            at = place_ref[0, (first + i) * spread + s]
            both = message_ref[pl.ds(s * record, record), :] * cur_ref[at]
            prod_ref[i * spread + s] = jnp.sum(both.reshape(-1, 8, LANES), axis=0)
    by_slot = jnp.sum(jnp.sum(prod_ref[...], axis=1), axis=1, keepdims=True)
    return jnp.sum((rates * by_slot).reshape(count // 8, 8, boxes), axis=0)


def add_slots(message_refs, first, slots, record, acc_ref, place_ref):
    for i, message_ref in enumerate(message_refs):
        for s in range(slots):
            at = place_ref[0, (first + i) * (LANES // LOW) + s]
            acc_ref[at] = acc_ref[at] + message_ref[pl.ds(s * record, record), :]


def sum_first_kernel(slots, high_count, *refs):
    message_refs, current_refs = refs[: LOW // 2], refs[LOW // 2 : LOW // 2 + high_count]
    acc_ref, cur_ref, extra_ref, share_ref, prod_ref, table_ref, place_ref, sem = refs[
        LOW // 2 + high_count :
    ]
    blocks, record = current_refs[0].shape[:2]
    extra = functools.reduce(jnp.add, [ref[pl.ds(slots * record, 8), :] for ref in message_refs])
    copy = start_places(extra, table_ref, place_ref, sem)
    for d in range(high_count):
        cur_ref[pl.ds(d * blocks, blocks)] = current_refs[d][...]
    acc_ref[...] = jnp.zeros(acc_ref.shape, jnp.float32)
    share_ref[...] = box_shares(
        message_refs, 0, slots, share_ref.shape[1], extra, cur_ref, prod_ref, place_ref, copy
    )
    add_slots(message_refs, 0, slots, record, acc_ref, place_ref)
    extra_ref[...] = extra


def sum_last_kernel(slots, high_count, blocks, norm_shape, *refs):
    message_refs, refs = refs[: LOW // 2], refs[LOW // 2 :]
    (first_ref, cur_ref, first_extra_ref, first_share_ref), refs = refs[:4], refs[4:]
    out_refs, (whole_grad_ref, acc_ref, *refs) = refs[:high_count], refs[high_count:]
    prod_ref, table_ref, place_ref, sem, grad_ref, grad_sem = refs
    record = cur_ref.shape[1]
    extra = functools.reduce(jnp.add, [ref[pl.ds(slots * record, 8), :] for ref in message_refs])
    copy = start_places(extra, table_ref, place_ref, sem)
    acc_ref[...] = first_ref[...]
    share = box_shares(
        message_refs, LOW // 2, slots, grad_ref.shape[2], extra, cur_ref, prod_ref, place_ref, copy
    )
    box_sums = jnp.sum(share + first_share_ref[...], axis=0, keepdims=True) * norm_shape
    grad_ref[...] = jnp.broadcast_to(box_sums[None], grad_ref.shape)
    copy = pltpu.make_async_copy(grad_ref, whole_grad_ref, grad_sem)
    copy.start()
    add_slots(message_refs, LOW // 2, slots, record, acc_ref, place_ref)
    extra = extra + first_extra_ref[...]
    for d in range(high_count):
        for b in range(blocks):
            out_refs[d][pl.ds(b * record, record), :] = acc_ref[d * blocks + b]
        for row in range(blocks * record, out_refs[d].shape[0], 8):
            out_refs[d][pl.ds(row, 8), :] = extra
    copy.wait()


def update_kernel(angles, norm_far, high_count, *refs):
    sum_refs = refs[:high_count]
    adjoint_ref, radiation_ref, inverse_ref, out_ref = refs[high_count:]
    blocks = inverse_ref.shape[0]
    stride = 2 * blocks
    record = 2 * angles

    def total(start, rows):
        return functools.reduce(jnp.add, [ref[pl.ds(start, rows), :] for ref in sum_refs])

    far = total(blocks * record, 8)[FAR_ROW : FAR_ROW + 1] * norm_far
    lane = lax.broadcasted_iota(jnp.int32, (angles, LANES), 1)
    angle = lax.broadcasted_iota(jnp.int32, (angles, LANES), 0)
    far_real = jnp.sum(jnp.where(lane == angle, far, 0.0), axis=1, keepdims=True)
    far_imag = jnp.sum(jnp.where(lane == angle + angles, far, 0.0), axis=1, keepdims=True)
    far_real = jnp.broadcast_to(far_real, (angles, LANES))
    far_imag = jnp.broadcast_to(far_imag, (angles, LANES))
    for block in range(blocks):
        rows_real = pl.ds(2 * block, angles, stride=stride)
        rows_imag = pl.ds(2 * block + 1, angles, stride=stride)
        near = total(block * record, record)
        rad_real, rad_imag = radiation_ref[rows_real, :], radiation_ref[rows_imag, :]
        real = (far_real * rad_real + far_imag * rad_imag - near[:angles]).astype(jnp.bfloat16)
        imag = (far_imag * rad_real - far_real * rad_imag - near[angles:]).astype(jnp.bfloat16)
        step = jnp.dot(complex_rows(real, imag), inverse_ref[block], preferred_element_type=jnp.float32)
        out_ref[rows_real, :] = adjoint_ref[rows_real, :] + step[:angles]
        out_ref[rows_imag, :] = adjoint_ref[rows_imag, :] + step[angles:]


def on_device(
    adjoint,
    currents,
    radiation,
    near_blocks,
    inverse_blocks,
    col_device,
    col_offset,
    box_of_block,
    pair_rate,
):
    angles, blocks, unknowns = adjoint.shape[1], adjoint.shape[2], adjoint.shape[4]
    near_count = near_blocks.shape[1]
    pairs = blocks * near_count
    record = 2 * angles
    basis_count = lax.axis_size("basis")
    high_count = basis_count // LOW
    angles_all = angles * lax.axis_size("angle")
    boxes = BOX_DEV * basis_count
    slots = 2 * pairs // basis_count * high_count
    vmem = pl.BlockSpec(memory_space=pltpu.VMEM)
    params = pltpu.CompilerParams(vmem_limit_bytes=VMEM_LIMIT)

    def moved(value, bits):
        return lax.ppermute(value, "basis", [(i, i ^ bits) for i in range(basis_count)])

    flat = (angles * blocks * 2, unknowns)
    adjoint_rows = adjoint.reshape(flat)
    currents_rows = currents.reshape(flat)
    radiation_rows = radiation.reshape(flat)
    near = near_blocks.reshape(pairs, 2 * unknowns, unknowns)
    inverse = inverse_blocks.reshape(blocks, 2 * unknowns, unknowns)
    f32 = functools.partial(jax.ShapeDtypeStruct, dtype=jnp.float32)
    message = f32((slots * record + 8, unknowns))
    inputs = (
        col_device,
        col_offset,
        box_of_block,
        pair_rate,
        adjoint_rows,
        currents_rows,
        radiation_rows,
        near,
    )
    *messages, own_currents = pl.pallas_call(
        functools.partial(fill_kernel, slots),
        out_shape=[message] * LOW + [f32((blocks, record, unknowns))],
        in_specs=[pl.BlockSpec(memory_space=pltpu.HBM)] * len(inputs),
        out_specs=[vmem] * (LOW + 1),
        scratch_shapes=[pltpu.SMEM(whole.shape, whole.dtype) for whole in inputs[:4]]
        + [pltpu.VMEM(whole.shape, whole.dtype) for whole in inputs[4:]]
        + [pltpu.VMEM((LOW * slots, record, unknowns), jnp.float32)]
        + [pltpu.SemaphoreType.DMA((7,)), pltpu.SemaphoreType.DMA((blocks,))],
        compiler_params=params,
        name="fill",
    )(*[pltpu.with_memory_space_constraint(whole, pltpu.HBM) for whole in inputs])
    arrived = [messages[0]] + [moved(messages[e], e) for e in range(1, LOW)]
    beside = [own_currents] + [moved(own_currents, d * LOW) for d in range(1, high_count)]
    box_lanes = -(-boxes // LANES) * LANES
    columns = f32((high_count * blocks, record, unknowns))
    half = LANES // 2
    tables = [
        pltpu.VMEM((half, 8, unknowns), jnp.float32),
        pltpu.VMEM((8, LANES), jnp.int32),
        pltpu.SMEM((8, LANES), jnp.int32),
        pltpu.SemaphoreType.DMA,
    ]
    first_sums = pl.pallas_call(
        functools.partial(sum_first_kernel, slots, high_count),
        out_shape=[columns, columns, f32((8, unknowns)), f32((8, box_lanes))],
        in_specs=[vmem] * (LOW // 2 + high_count),
        out_specs=[vmem] * 4,
        scratch_shapes=tables,
        compiler_params=params,
        name="sum_first",
    )(*arrived[: LOW // 2], *beside)
    partials = [f32((blocks * record + 8 * (1 + min(d // 2, 1)), unknowns)) for d in range(high_count)]
    everyone = ("basis", "pol")
    senders = basis_count * lax.axis_size("pol")
    norm_shape = -1.0 / math.sqrt(4 * unknowns * angles_all * near_count)
    *sums, grad = pl.pallas_call(
        functools.partial(sum_last_kernel, slots, high_count, blocks, norm_shape),
        out_shape=partials + [f32((senders, 1, box_lanes))],
        in_specs=[vmem] * (LOW // 2 + 4),
        out_specs=[vmem] * high_count + [pl.BlockSpec(memory_space=pltpu.HBM)],
        scratch_shapes=[pltpu.VMEM(columns.shape, jnp.float32)]
        + tables
        + [pltpu.VMEM((senders, 1, box_lanes), jnp.float32), pltpu.SemaphoreType.DMA],
        compiler_params=params,
        name="sum_last",
    )(*arrived[LOW // 2 :], *first_sums)
    totals = [sums[0]] + [moved(sums[d], d * LOW) for d in range(1, high_count)]
    norm_far = 1.0 / math.sqrt(blocks * basis_count * unknowns)
    updated = pl.pallas_call(
        functools.partial(update_kernel, angles, norm_far, high_count),
        out_shape=f32(flat),
        in_specs=[vmem] * (high_count + 3),
        out_specs=vmem,
        compiler_params=params,
        name="update",
    )(*totals, adjoint_rows, radiation_rows, inverse)
    gathered = lax.all_to_all(grad, everyone, split_axis=0, concat_axis=0)
    gathered, updated = lax.optimization_barrier((gathered, updated))
    mine = lax.dynamic_slice_in_dim(gathered, lax.axis_index("basis") * BOX_DEV, BOX_DEV, axis=2)
    share = jnp.sum(mine[:, 0], axis=0)
    if lax.axis_size("angle") > 1:
        share = lax.psum(share, "angle")
    return (updated.reshape(adjoint.shape), share)


def solution(mesh):
    placed = (
        P("pol", "angle", "basis", None, None),
        P("pol", "angle", "basis", None, None),
        P("pol", "angle", "basis", None, None),
        P("basis", None, None, None, None),
        P("basis", None, None, None),
        P("basis", None),
        P("basis", None),
        P("basis"),
        P("basis", None),
    )
    return jax.shard_map(
        on_device,
        mesh=mesh,
        in_specs=placed,
        out_specs=(P("pol", "angle", "basis", None, None), P("basis")),
        check_vma=False,
    )
```
